32 devices in a mesh: rep: 4 (over y, x), fsdp: 8 (over z, core).
Axes of the slice: x: 2, y: 2, z: 4, core: 2. Of those that a mesh axis runs over, the one named last changes fastest.
Arguments:
- tokens: bfloat16 [2, 32, 512, 768], P(None, ('rep', 'fsdp')), may hold values from -6 to 6
- lengths: int32 [2, 32], P(None, ('rep', 'fsdp')), may hold values from 128 to 512, as said below
- boundary: int32 [2, 32], P(None, ('rep', 'fsdp')), may hold values from 1 to 511, as said below
- w_query: bfloat16 [768, 768], P('fsdp'), may hold values from -0.21875 to 0.21875
- b_query: bfloat16 [768], P('fsdp'), may hold values from -2.5 to 2.5
- w_key: bfloat16 [768, 768], P('fsdp'), may hold values from -0.21875 to 0.21875
- b_key: bfloat16 [768], P('fsdp'), may hold values from -2.5 to 2.5
- w_value: bfloat16 [768, 768], P('fsdp'), may hold values from -0.21875 to 0.21875
- b_value: bfloat16 [768], P('fsdp'), may hold values from -2.5 to 2.5
- w_out: bfloat16 [768, 768], P('fsdp'), may hold values from -1.75 to 1.75
- b_out: bfloat16 [768], P('fsdp'), may hold values from -2.5 to 2.5
- first_gain: bfloat16 [768], P('fsdp'), may hold values from 0.5 to 1.5
- first_shift: bfloat16 [768], P('fsdp'), may hold values from -2.5 to 2.5
- w_up: bfloat16 [768, 3072], P('fsdp'), may hold values from -0.21875 to 0.21875
- b_up: bfloat16 [3072], P('fsdp'), may hold values from -2.5 to 2.5
- w_down: bfloat16 [3072, 768], P('fsdp'), may hold values from -0.109375 to 0.109375
- b_down: bfloat16 [768], P('fsdp'), may hold values from -2.5 to 2.5
- second_gain: bfloat16 [768], P('fsdp'), may hold values from 0.5 to 1.5
- second_shift: bfloat16 [768], P('fsdp'), may hold values from -2.5 to 2.5
- rel_table: bfloat16 [512, 768], P('fsdp'), may hold values from -6 to 6
- type_table: bfloat16 [2, 768], P(None, 'fsdp'), may hold values from -3 to 3
- out_grad: bfloat16 [2, 32, 512, 768], P(None, ('rep', 'fsdp')), may hold values from -6 to 6
Outputs:
- layer_out: bfloat16 [2, 32, 512, 768], P(None, ('rep', 'fsdp'))
- tokens_grad: bfloat16 [2, 32, 512, 768], P(None, ('rep', 'fsdp'))
- grad_w_query: float32 [768, 768], P('fsdp')
- grad_b_query: float32 [768], P('fsdp')
- grad_w_key: float32 [768, 768], P('fsdp')
- grad_b_key: float32 [768], P('fsdp')
- grad_w_value: float32 [768, 768], P('fsdp')
- grad_b_value: float32 [768], P('fsdp')
- grad_w_out: float32 [768, 768], P('fsdp')
- grad_b_out: float32 [768], P('fsdp')
- grad_first_gain: float32 [768], P('fsdp')
- grad_first_shift: float32 [768], P('fsdp')
- grad_w_up: float32 [768, 3072], P('fsdp')
- grad_b_up: float32 [3072], P('fsdp')
- grad_w_down: float32 [3072, 768], P('fsdp')
- grad_b_down: float32 [768], P('fsdp')
- grad_second_gain: float32 [768], P('fsdp')
- grad_second_shift: float32 [768], P('fsdp')
- grad_rel_table: float32 [512, 768], P('fsdp')
- grad_type_table: float32 [2, 768], P(None, 'fsdp')
The draws below stay inside these ranges and needn't reach their ends.
Inputs may be any that keep to these rules, and one draw needn't show every extreme that they name: `lengths`: each sequence's valid tokens come first; the largest entry is exactly 512 and the smallest exactly 128 in every draw. `boundary`: lies below its sequence's valid length; both ends of the range are reached in every draw.
All inputs are finite; a program needn't handle non-finite values.
Results may differ from the reference program's by a relative error of at most 0.03.
Values may be sent and summed in bfloat16 or wider, within the bound.
No kernel may reach another device: no remote copies, remote signals or barrier semaphores. Data moves between devices by JAX's collectives and lax.ppermute only.
A program may use at most 320 MiB of HBM per device.

```python
import math
import jax
import jax.numpy as jnp
import numpy as np
from jax import lax

D = 768
HEADS = 12
HEAD_DIM = 64
FF = 3072
BUCKETS = 256
MAX_POS = 512
SEQ_LEN = 512
MICRO = 2
SEQ_DEV = 1
SEQS = 32


def paired_draws(key):
    count = MICRO * SEQS
    lengths = jax.random.randint(jax.random.fold_in(key, 101), (count,), SEQ_LEN // 4, SEQ_LEN + 1)
    first = jax.random.randint(jax.random.fold_in(key, 102), (), 0, count)
    second = (first + 1 + jax.random.randint(jax.random.fold_in(key, 103), (), 0, count - 1)) % count
    places = jnp.arange(count)
    lengths = jnp.where(places == first, SEQ_LEN, lengths)
    lengths = jnp.where(places == second, SEQ_LEN // 4, lengths)
    spread = jax.random.randint(jax.random.fold_in(key, 104), (count,), 0, 1048576)
    boundary = 1 + spread % (lengths - 1)
    boundary = jnp.where(places == first, SEQ_LEN - 1, boundary)
    boundary = jnp.where(places == second, 1, boundary)
    return (lengths.reshape(MICRO, SEQS).astype(jnp.int32), boundary.reshape(MICRO, SEQS).astype(jnp.int32))


def draw_lengths(key, part):
    return paired_draws(key)[0]


def draw_boundary(key, part):
    return paired_draws(key)[1]


def level_of(rng, extent, cuts, low, largest):
    factor_of = 1.0
    for axis_at, parts in cuts:
        heights = jax.random.uniform(jax.random.fold_in(jax.random.fold_in(rng, 6), axis_at), (parts,), jnp.float32, low / len(cuts), largest / len(cuts))
        factor_of = factor_of * jnp.repeat(jnp.exp(heights), extent[axis_at] // parts).reshape((-1,) + (1,) * (len(extent) - 1 - axis_at))
    return factor_of


def normal_values(rng, dims, scale, reach, split=(), held_as=jnp.bfloat16):
    level = level_of(rng, dims, split, -0.22, 0.18) if split else 1.0
    values = jax.random.normal(rng, dims, jnp.float32) * scale * level
    return jnp.minimum(jnp.maximum(values, -reach), reach).astype(held_as)


def setup_inputs(seed: int = 0) -> dict:
    key_list = jax.random.split(jax.random.key(seed), 23)
    tokens = normal_values(key_list[0], (MICRO, SEQS, SEQ_LEN, D), 1.0, 6.0, ((1, 32),))
    lengths = draw_lengths(jax.random.fold_in(key_list[22], 71), 0)
    boundary = draw_boundary(jax.random.fold_in(key_list[22], 71), 0)
    w_query = normal_values(key_list[3], (D, D), D ** -0.5, 0.21875, ((0, 8),))
    b_query = normal_values(key_list[4], (D,), 0.3, 2.5, ((0, 8),))
    w_key = normal_values(key_list[5], (D, D), D ** -0.5, 0.21875, ((0, 8),))
    b_key = normal_values(key_list[6], (D,), 0.3, 2.5, ((0, 8),))
    w_value = normal_values(key_list[7], (D, D), D ** -0.5, 0.21875, ((0, 8),))
    b_value = normal_values(key_list[8], (D,), 0.3, 2.5, ((0, 8),))
    w_out = normal_values(key_list[9], (D, D), (D // 64) ** -0.5, 1.75, ((0, 8),))
    b_out = normal_values(key_list[10], (D,), 0.3, 2.5, ((0, 8),))
    first_gain = jnp.clip(1.0 + 0.1 * jax.random.normal(key_list[11], (D,), jnp.float32), 0.5, 1.5).astype(jnp.bfloat16)
    first_shift = normal_values(key_list[12], (D,), 0.3, 2.5, ((0, 8),))
    w_up = normal_values(key_list[13], (D, FF), D ** -0.5, 0.21875, ((0, 8),))
    b_up = normal_values(key_list[14], (FF,), 0.3, 2.5, ((0, 8),))
    w_down = normal_values(key_list[15], (FF, D), FF ** -0.5, 0.109375, ((0, 8),))
    b_down = normal_values(key_list[16], (D,), 0.3, 2.5, ((0, 8),))
    second_gain = jnp.clip(1.0 + 0.1 * jax.random.normal(key_list[17], (D,), jnp.float32), 0.5, 1.5).astype(jnp.bfloat16)
    second_shift = normal_values(key_list[18], (D,), 0.3, 2.5, ((0, 8),))
    rel_table = normal_values(key_list[19], (2 * BUCKETS, D), 1.0, 6.0, ((0, 8),))
    type_table = normal_values(key_list[20], (2, D), 0.5, 3.0, ((1, 8),))
    out_grad = normal_values(key_list[21], (MICRO, SEQS, SEQ_LEN, D), 1.0, 6.0, ((1, 32),))
    return {"tokens": tokens, "lengths": lengths, "boundary": boundary, "w_query": w_query, "b_query": b_query, "w_key": w_key, "b_key": b_key, "w_value": w_value, "b_value": b_value, "w_out": w_out, "b_out": b_out, "first_gain": first_gain, "first_shift": first_shift, "w_up": w_up, "b_up": b_up, "w_down": w_down, "b_down": b_down, "second_gain": second_gain, "second_shift": second_shift, "rel_table": rel_table, "type_table": type_table, "out_grad": out_grad}


NORM_EPS = 1e-07
MASKED = -1e+30

@jax.custom_vjp
def low(v):
    return lax.optimization_barrier(v.astype(jnp.bfloat16)).astype(jnp.float32)

@jax.custom_vjp
def low_back(v):
    return v

def low_keep(v):
    return (low(v), None)

def low_pass(kept, grad):
    return (grad,)

def back_keep(v):
    return (v, None)

def back_low(kept, grad):
    return (low(grad),)
low.defvjp(low_keep, low_pass)
low_back.defvjp(back_keep, back_low)

def bucket_index(offset_of):
    middle = BUCKETS // 2
    sign_of = np.sign(offset_of)
    magnitude = np.where((offset_of < middle) & (offset_of > -middle), middle - 1, np.abs(offset_of))
    log_pos = np.ceil(np.log(magnitude / middle) / np.log((MAX_POS - 1) / middle) * (middle - 1)) + middle
    bucket = np.where(magnitude <= middle, offset_of, log_pos * sign_of)
    return np.clip(bucket + BUCKETS, 0, 2 * BUCKETS - 1)

def offset_tables(seq_len):
    offsets = np.arange(2 * seq_len)
    table_rows = np.arange(2 * BUCKETS)
    from_query = bucket_index(seq_len - 1 - offsets)
    from_key = bucket_index(offsets - seq_len + 1)
    pick_query = (from_query[:, None] == table_rows[None, :]).astype(np.float32)
    pick_key = (from_key[:, None] == table_rows[None, :]).astype(np.float32)
    return (pick_query, pick_key)

def realign(scores_block):
    leading = scores_block.shape[:-2]
    row_count = scores_block.shape[-2]
    columns = scores_block.shape[-1]
    flattened = scores_block.reshape(leading + (row_count * columns,))
    flattened = flattened[..., row_count - 1:row_count - 1 + row_count * (columns - 1)]
    return flattened.reshape(leading + (row_count, columns - 1))[..., :row_count]

def normalize(values):
    centred = values - lax.optimization_barrier(jnp.mean(values, -1, keepdims=True))
    inverse = lax.rsqrt(lax.optimization_barrier(jnp.mean(centred * centred, -1, keepdims=True)) + NORM_EPS)
    return centred * inverse

def matmul(left_side, right_side):
    return jnp.dot(left_side, right_side, precision=lax.Precision.HIGHEST, preferred_element_type=jnp.float32)

def heads_of(values, seq_count):
    return values.reshape(seq_count, SEQ_LEN, HEADS, HEAD_DIM).transpose(0, 2, 1, 3)

def group_layer(weights, key_offsets, query_offsets, tokens, lengths, boundary):
    w_query, b_query, w_key, b_key, w_value, b_value, w_out, b_out, first_gain, first_shift, w_up, b_up, w_down, b_down, second_gain, second_shift, rel_table, type_table = weights
    highest = lax.Precision.HIGHEST
    seq_count = tokens.shape[0]
    row_count = seq_count * SEQ_LEN
    key_offsets = low_back(key_offsets)
    query_offsets = low_back(query_offsets)
    positions = jnp.arange(SEQ_LEN)
    second_part = (positions[None, :] >= boundary[:, None]).reshape(row_count, 1)
    summed = tokens.reshape(row_count, D) + jnp.where(second_part, type_table[1], type_table[0])
    summed_low = low(summed)
    queries = heads_of(low(low_back(matmul(summed_low, w_query) + b_query)), seq_count)
    key_heads = heads_of(low(low_back(matmul(summed_low, w_key) + b_key)), seq_count)
    value_heads = heads_of(low(low_back(matmul(summed_low, w_value) + b_value)), seq_count)
    key_table = key_offsets.reshape(2 * SEQ_LEN, HEADS, HEAD_DIM).transpose(1, 0, 2)
    query_table = query_offsets.reshape(2 * SEQ_LEN, HEADS, HEAD_DIM).transpose(1, 0, 2)
    direct = jnp.einsum('shid,shjd->shij', queries, key_heads, precision=highest)
    from_query = realign(jnp.einsum('shid,hkd->shik', queries, key_table, precision=highest))
    from_key = jnp.swapaxes(realign(jnp.einsum('shjd,hkd->shjk', key_heads, query_table, precision=highest)), -1, -2)
    raw_scores = low_back(direct + from_query + from_key)
    key_valid = positions[None, :] < lengths[:, None]
    scaling = 1.0 / math.sqrt(3 * HEAD_DIM)
    scores = jnp.where(key_valid[:, None, None, :], raw_scores * scaling, MASKED)
    soft_probs = jax.nn.softmax(scores, axis=-1) * key_valid.astype(jnp.float32)[:, None, :, None]
    context = low(low_back(jnp.einsum('shij,shjd->shid', low(soft_probs), value_heads, precision=highest)))
    context = context.transpose(0, 2, 1, 3).reshape(row_count, D)
    attended = low_back(matmul(context, w_out) + b_out)
    hidden = normalize(summed + attended) * first_gain + first_shift
    raised = low_back(matmul(low(hidden), w_up) + b_up)
    active = low(jax.nn.gelu(raised, approximate=False))
    mixed_sum = hidden + low_back(matmul(active, w_down) + b_down)
    return (normalize(mixed_sum) * second_gain + second_shift).reshape(seq_count, SEQ_LEN, D)

def micro_layer(weights, inputs, lengths, boundary, pick_query, pick_key, checkpointed):
    w_query = weights[0]
    b_query = weights[1]
    w_key = weights[2]
    b_key = weights[3]
    rel_table = weights[16]
    pos_key = low(matmul(rel_table, w_key) + b_key)
    pos_query = low(matmul(rel_table, w_query) + b_query)
    key_offsets = matmul(pick_query, pos_key)
    query_offsets = matmul(pick_key, pos_query)
    groups = SEQS // SEQ_DEV

    def one_group(per_group):
        group_tokens, group_lengths, group_bound = per_group
        return checkpointed(weights, key_offsets, query_offsets, group_tokens, group_lengths, group_bound)
    shaped = inputs.reshape(groups, SEQ_DEV, SEQ_LEN, D)
    result = lax.map(one_group, (shaped, lengths.reshape(groups, SEQ_DEV), boundary.reshape(groups, SEQ_DEV)))
    return result.reshape(SEQS, SEQ_LEN, D)

def reference(tokens, lengths, boundary, w_query, b_query, w_key, b_key, w_value, b_value, w_out, b_out, first_gain, first_shift, w_up, b_up, w_down, b_down, second_gain, second_shift, rel_table, type_table, out_grad):
    weights = tuple([initial.astype(jnp.float32) for initial in (w_query, b_query, w_key, b_key, w_value, b_value, w_out, b_out, first_gain, first_shift, w_up, b_up, w_down, b_down, second_gain, second_shift, rel_table, type_table)])
    pick_c, pick_p = offset_tables(SEQ_LEN)
    pick_query = jnp.asarray(pick_c, jnp.float32)
    pick_key = jnp.asarray(pick_p, jnp.float32)
    checkpointed = jax.checkpoint(group_layer)

    def forward(weight_set, inputs):
        results = []
        for micro_index in range(MICRO):
            results.append(micro_layer(weight_set, inputs[micro_index], lengths[micro_index], boundary[micro_index], pick_query, pick_key, checkpointed))
        return jnp.stack(results)
    layer_out, pull_back = jax.vjp(forward, weights, tokens.astype(jnp.float32))
    grad_weights, grad_tokens = pull_back(out_grad.astype(jnp.float32))
    return (layer_out.astype(jnp.bfloat16), grad_tokens.astype(jnp.bfloat16), grad_weights[0], grad_weights[1], grad_weights[2], grad_weights[3], grad_weights[4], grad_weights[5], grad_weights[6], grad_weights[7], grad_weights[8], grad_weights[9], grad_weights[10], grad_weights[11], grad_weights[12], grad_weights[13], grad_weights[14], grad_weights[15], grad_weights[16], grad_weights[17])
```

```python
import math

import jax
import jax.numpy as jnp
import numpy as np
from jax import lax
from jax.experimental import pallas as pl
from jax.experimental.pallas import tpu as pltpu
from jax.sharding import PartitionSpec as P

BUCKETS = 256
MAX_POS = 512
NORM_EPS = 1e-07

HEAD_DIM=64
MASKED=-1e30
f32=jnp.float32; bf=jnp.bfloat16
BLK=128
LOG2E=math.log2(math.e)

def nn(a,b): return lax.dot_general(a,b,(((1,),(0,)),((),())),preferred_element_type=f32)
def nt(a,b): return lax.dot_general(a,b,(((1,),(1,)),((),())),preferred_element_type=f32)

def eye(rows, flip=False):
    r=lax.broadcasted_iota(jnp.int32,(rows,rows),0)
    c=lax.broadcasted_iota(jnp.int32,(rows,rows),1)
    return jnp.where((r+c==rows-1) if flip else (r==c),1.0,0.0).astype(bf)

def attn_fwd_kernel(len_ref,q_ref,k_ref,v_ref,pkr_ref,pq_ref,ctxT_ref,p_ref,linv_ref,c_scr,s_scr):
    S=q_ref.shape[0]
    nb=S//BLK
    W=S+BLK
    m=pl.program_id(1)
    length=len_ref[m]
    scale=LOG2E/math.sqrt(3*HEAD_DIM)
    q=q_ref[...]; k=k_ref[...]
    pq=pq_ref[...]
    vT=v_ref[...].T
    ident=eye(BLK)
    lane_s=lax.broadcasted_iota(jnp.int32,(S,2*HEAD_DIM),1)
    row_s=lax.broadcasted_iota(jnp.int32,(S,2*HEAD_DIM),0)
    lane_t=lax.broadcasted_iota(jnp.int32,(2*S,2*HEAD_DIM),1)
    bias=jnp.where(row_s<length,0.0,MASKED).astype(bf)
    zero=jnp.zeros((),bf)
    pos=lax.broadcasted_iota(jnp.int32,(1,S),1)
    for h in range(2):
        mine=(lane_s<HEAD_DIM) if h==0 else (lane_s>=HEAD_DIM)
        mine_t=(lane_t<HEAD_DIM) if h==0 else (lane_t>=HEAD_DIM)
        spare=HEAD_DIM if h==0 else 0
        qh=jnp.where(mine,q,zero)
        kb=jnp.where(mine,k,jnp.where(lane_s==spare,bias,zero))
        pqh=jnp.where(mine_t,pq,jnp.where(lane_t==spare,jnp.ones((),bf),zero))
        for b in range(nb):
            st=(nb-1-b)*BLK
            c=nt(qh[b*BLK:(b+1)*BLK],pkr_ref[st:st+W,:]).astype(bf)
            c_scr[b*BLK:(b+1)*BLK,:]=pltpu.roll(c,S+1,1,stride=1,stride_axis=0)[:,:S]
        top=None
        for b in range(nb):
            st=(nb-1-b)*BLK
            js=slice(b*BLK,(b+1)*BLK)
            d=nt(kb[js],pqh[st:st+W]).astype(bf)
            d=pltpu.roll(d,S+1,1,stride=1,stride_axis=0)[:,:S]
            lhs=jnp.concatenate([k[js],ident],axis=1)
            rhs=jnp.concatenate([qh,c_scr[:,js]],axis=1)
            s=nt(lhs,rhs)+d.astype(f32)
            s_scr[js,:]=s
            t=jnp.max(s,axis=0,keepdims=True)
            top=t if top is None else jnp.maximum(top,t)
        top=top*scale
        tot=None
        for b in range(nb):
            js=slice(b*BLK,(b+1)*BLK)
            p=jnp.exp2(s_scr[js,:]*scale-top)
            t=jnp.sum(p,axis=0,keepdims=True)
            tot=t if tot is None else tot+t
            p_ref[0,h,js,:]=p.astype(bf)
        linv=jnp.where(pos<length,1.0/tot,0.0)
        linv_ref[0,0,h:h+1,:]=linv
        ctx=nn(vT[h*HEAD_DIM:(h+1)*HEAD_DIM,:],p_ref[0,h])*linv
        ctxT_ref[h*HEAD_DIM:(h+1)*HEAD_DIM,:]=ctx.astype(bf)

def attn_fwd(qkv,pkr,pq,lengths,heads):
    M=lengths.shape[0]; D=heads*HEAD_DIM
    S=pq.shape[0]//2
    NP=heads//2; L=2*HEAD_DIM
    grid=(NP,M)
    return pl.pallas_call(
        attn_fwd_kernel,
        grid_spec=pltpu.PrefetchScalarGridSpec(
            num_scalar_prefetch=1,grid=grid,
            in_specs=[
                pl.BlockSpec((S,L),lambda p,m,_:(m,p)),
                pl.BlockSpec((S,L),lambda p,m,_:(m,NP+p)),
                pl.BlockSpec((S,L),lambda p,m,_:(m,2*NP+p)),
                pl.BlockSpec((2*S,L),lambda p,m,_:(0,p)),
                pl.BlockSpec((2*S,L),lambda p,m,_:(0,p)),
            ],
            out_specs=[
                pl.BlockSpec((L,S),lambda p,m,_:(p,m)),
                pl.BlockSpec((1,2,S,S),lambda p,m,_:(m,p,0,0)),
                pl.BlockSpec((1,1,2,S),lambda p,m,_:(m,p,0,0)),
            ],
            scratch_shapes=[pltpu.VMEM((S,S),bf),pltpu.VMEM((S,S),f32)],
        ),
        out_shape=[jax.ShapeDtypeStruct((D,M*S),bf),jax.ShapeDtypeStruct((M,heads,S,S),bf),jax.ShapeDtypeStruct((M,NP,2,S),f32)],
        compiler_params=pltpu.CompilerParams(vmem_limit_bytes=40*1024*1024),
        cost_estimate=pl.CostEstimate(flops=int(2*M*heads*S*S*64*12),bytes_accessed=int(M*heads*S*S*2),transcendentals=M*heads*S*S),
    )(lengths,qkv,qkv,qkv,pkr,pq)

def attn_bwd_kernel(q_ref,k_ref,v_ref,dcT_ref,ctxT_ref,p_ref,linv_ref,pk_ref,pq_ref,dq_ref,dk_ref,dv_ref,ko_ref,qo_ref,ds_scr):
    S=q_ref.shape[0]
    nb=S//BLK
    W=S+BLK
    m=pl.program_id(1)
    scale=1.0/math.sqrt(3*HEAD_DIM)
    zero=jnp.zeros((),bf)
    ident=eye(BLK); flip=eye(BLK,True)
    q=q_ref[...]
    def reverse(x):
        return jnp.concatenate([nn(flip,x[(nb-1-b)*BLK:(nb-b)*BLK]).astype(bf) for b in range(nb)],axis=0)
    kr=reverse(k_ref[...]); vr=reverse(v_ref[...])
    qT=q.T; krT=kr.T
    lane_s=lax.broadcasted_iota(jnp.int32,(S,2*HEAD_DIM),1)
    lane_t=lax.broadcasted_iota(jnp.int32,(2*S,2*HEAD_DIM),1)
    pad=jnp.zeros((BLK,BLK),bf)
    @pl.when(m==0)
    def _():
        ko_ref[...]=jnp.zeros_like(ko_ref)
        qo_ref[...]=jnp.zeros_like(qo_ref)
    dq=[None]*nb; dk=[None]*nb; dv=None
    zrow=jnp.zeros((HEAD_DIM,S),bf)
    for h in range(2):
        hs=slice(h*HEAD_DIM,(h+1)*HEAD_DIM)
        mine=(lane_s<HEAD_DIM) if h==0 else (lane_s>=HEAD_DIM)
        mine_t=(lane_t<HEAD_DIM) if h==0 else (lane_t>=HEAD_DIM)
        qh=jnp.where(mine,q,zero); krh=jnp.where(mine,kr,zero)
        pkh=jnp.where(mine_t,pk_ref[...],zero); pqh=jnp.where(mine_t,pq_ref[...],zero)
        linv=linv_ref[0,0,h:h+1,:]
        dc=dcT_ref[hs,:].astype(f32)*linv
        delta=jnp.sum(dc*ctxT_ref[hs,:].astype(f32),axis=0,keepdims=True)*scale
        dcl=dc.astype(bf); dcs=(dc*scale).astype(bf)
        def wide(x): return jnp.concatenate([x,zrow] if h==0 else [zrow,x],axis=0)
        t=nt(p_ref[0,h],wide(dcl))
        dv=t if dv is None else dv+t
        dcw=wide(dcs)
        for b in range(nb):
            js=slice(b*BLK,(b+1)*BLK)
            dp=nn(vr[js],dcw)
            p=nn(flip,p_ref[0,h,(nb-1-b)*BLK:(nb-b)*BLK,:])
            ds=(p*(dp-delta)).astype(bf)
            ds_scr[js,:]=ds
            far=pltpu.roll(jnp.concatenate([ds,pad],axis=1),0,1,stride=1,stride_axis=0)
            st=b*BLK
            t=nn(ds,qh)+nn(far,pqh[st:st+W])
            dk[b]=t if dk[b] is None else dk[b]+t
            qo_ref[hs,st:st+W]+=nn(krT[hs,js],far)
        for b in range(nb):
            js=slice(b*BLK,(b+1)*BLK)
            ds=nt(ident,ds_scr[:,js]).astype(bf)
            near=pltpu.roll(jnp.concatenate([ds,pad],axis=1),0,1,stride=1,stride_axis=0)
            st=b*BLK
            t=nn(ds,krh)+nn(near,pkh[st:st+W])
            dq[b]=t if dq[b] is None else dq[b]+t
            ko_ref[hs,st:st+W]+=nn(qT[hs,js],near)
    dv_ref[...]=dv.astype(bf)
    for b in range(nb):
        dq_ref[b*BLK:(b+1)*BLK,:]=dq[b].astype(bf)
        dk_ref[(nb-1-b)*BLK:(nb-b)*BLK,:]=nn(flip,dk[b].astype(bf)).astype(bf)

def attn_bwd(qkv,dcT,ctxT,p,linv,pk,pq):
    M,heads,S,_=p.shape; D=heads*HEAD_DIM
    NP=heads//2; L=2*HEAD_DIM
    tok=lambda off: pl.BlockSpec((S,L),lambda p,m:(m,off+p))
    colT=pl.BlockSpec((L,S),lambda p,m:(p,m))
    tab=pl.BlockSpec((2*S,L),lambda p,m:(0,p))
    return pl.pallas_call(
        attn_bwd_kernel,
        grid=(NP,M),
        in_specs=[tok(0),tok(NP),tok(2*NP),colT,colT,
            pl.BlockSpec((1,2,S,S),lambda p,m:(m,p,0,0)),
            pl.BlockSpec((1,1,2,S),lambda p,m:(m,p,0,0)),
            tab,tab],
        out_specs=[tok(0),tok(0),tok(0),pl.BlockSpec((L,2*S),lambda p,m:(p,0)),pl.BlockSpec((L,2*S),lambda p,m:(p,0))],
        out_shape=[jax.ShapeDtypeStruct((M*S,D),bf)]*3+[jax.ShapeDtypeStruct((D,2*S),f32)]*2,
        scratch_shapes=[pltpu.VMEM((S,S),bf)],
        compiler_params=pltpu.CompilerParams(vmem_limit_bytes=40*1024*1024),
        cost_estimate=pl.CostEstimate(flops=int(2*M*heads*S*S*64*24),bytes_accessed=int(M*heads*S*S*2),transcendentals=0),
    )(qkv,qkv,qkv,dcT,ctxT,p,linv,pk,pq)


def bucket_index(offset_of):
    middle = BUCKETS // 2
    sign_of = np.sign(offset_of)
    magnitude = np.where(
        (offset_of < middle) & (offset_of > -middle), middle - 1, np.abs(offset_of)
    )
    log_pos = (
        np.ceil(np.log(magnitude / middle) / np.log((MAX_POS - 1) / middle) * (middle - 1)) + middle
    )
    bucket = np.where(magnitude <= middle, offset_of, log_pos * sign_of)
    return np.clip(bucket + BUCKETS, 0, 2 * BUCKETS - 1)


def pick_rows(offsets):
    return (bucket_index(offsets)[:, None] == np.arange(2 * BUCKETS)[None, :]).astype(np.float32)


def tn(a, b):
    return lax.dot_general(a, b, (((0,), (0,)), ((), ())), preferred_element_type=f32)


def normalize(values):
    centred = values - jnp.mean(values, -1, keepdims=True)
    inverse = lax.rsqrt(jnp.mean(centred * centred, -1, keepdims=True) + NORM_EPS)
    return centred * inverse, inverse


def normalize_back(grad, normed, inverse):
    return inverse * (
        grad
        - jnp.mean(grad, -1, keepdims=True)
        - normed * jnp.mean(grad * normed, -1, keepdims=True)
    )


def gelu_slope(values):
    cumulative = 0.5 * (1.0 + lax.erf(values * (1.0 / math.sqrt(2.0))))
    density = jnp.exp(-0.5 * values * values) * (1.0 / math.sqrt(2.0 * math.pi))
    return cumulative + values * density


def per_device(
    tokens, lengths, boundary,
    w_query, b_query, w_key, b_key, w_value, b_value, w_out, b_out,
    first_gain, first_shift, w_up, b_up, w_down, b_down,
    second_gain, second_shift, rel_table, type_table, out_grad,
):
    micros, seqs, seq_len, features = tokens.shape
    rows = micros * seqs * seq_len
    heads = features // HEAD_DIM
    gather = lambda a: lax.all_gather(a, "fsdp", axis=0, tiled=True)
    vectors = (b_query, b_key, b_value, b_out, first_gain, first_shift, b_up, b_down,
               second_gain, second_shift, type_table[0], type_table[1])
    sizes = [v.shape[0] for v in vectors]
    packed = gather(jnp.concatenate(vectors)[None, :])
    ends = np.cumsum([0] + sizes)
    wide = [packed[:, a:b].reshape(-1).astype(f32) for a, b in zip(ends[:-1], ends[1:])]
    (v_query, v_key, v_value, v_out, g_first, s_first, v_up, v_down, g_second, s_second,
     type_zero, type_one) = wide
    w_qkv = gather(jnp.concatenate([w_query, w_key, w_value], axis=1))
    rel = gather(rel_table)
    w_o = gather(w_out)
    w_u = gather(w_up)
    w_d = gather(w_down)

    offsets = np.clip(np.arange(2 * seq_len) - (seq_len - 1), 1 - seq_len, seq_len - 1)
    pick = jnp.asarray(pick_rows(offsets), bf)
    pick_back = jnp.asarray(pick_rows(-offsets), bf)

    positions = jnp.arange(seq_len)
    second_part = (positions[None, None, :] >= boundary[:, :, None]).reshape(rows, 1)
    summed = tokens.reshape(rows, features).astype(f32) + jnp.where(second_part, type_one, type_zero)
    summed_low = summed.astype(bf)
    v_qkv = jnp.concatenate([v_query, v_key, v_value])
    qkv = (nn(summed_low, w_qkv) + v_qkv).astype(bf)
    pos = (nn(rel, w_qkv[:, : 2 * features]) + v_qkv[: 2 * features]).astype(bf)
    pos_query, pos_key = pos[:, :features], pos[:, features:]
    key_rows = nn(pick, pos_key).astype(bf)
    key_rows_back = nn(pick_back, pos_key).astype(bf)
    query_rows = nn(pick, pos_query).astype(bf)
    flat_lengths = lengths.reshape(-1)
    context_t, probs, inverse_total = attn_fwd(qkv, key_rows_back, query_rows, flat_lengths, heads)
    attended = tn(context_t, w_o) + v_out
    first_normed, first_inverse = normalize(summed + attended)
    hidden = first_normed * g_first + s_first
    hidden_low = hidden.astype(bf)
    raised = nn(hidden_low, w_u) + v_up
    active = jax.nn.gelu(raised, approximate=False).astype(bf)
    second_normed, second_inverse = normalize(hidden + nn(active, w_d) + v_down)
    layer_out = (second_normed * g_second + s_second).astype(bf).reshape(tokens.shape)

    grad_output = out_grad.reshape(rows, features).astype(f32)
    d_second_gain = jnp.sum(grad_output * second_normed, 0)
    d_second_shift = jnp.sum(grad_output, 0)
    grad_mixed = normalize_back(grad_output * g_second, second_normed, second_inverse)
    grad_ffn = grad_mixed.astype(bf)
    d_w_down = tn(active, grad_ffn)
    d_b_down = jnp.sum(grad_ffn.astype(f32), 0)
    grad_raised = (nt(grad_ffn, w_d) * gelu_slope(raised)).astype(bf)
    d_w_up = tn(hidden_low, grad_raised)
    d_b_up = jnp.sum(grad_raised.astype(f32), 0)
    grad_hidden = nt(grad_raised, w_u) + grad_mixed
    d_first_gain = jnp.sum(grad_hidden * first_normed, 0)
    d_first_shift = jnp.sum(grad_hidden, 0)
    grad_first = normalize_back(grad_hidden * g_first, first_normed, first_inverse)
    grad_attended = grad_first.astype(bf)
    d_w_out = nn(context_t, grad_attended)
    d_b_out = jnp.sum(grad_attended.astype(f32), 0)
    grad_context_t = nt(w_o, grad_attended).astype(bf)
    d_query, d_key, d_value, key_off, query_off = attn_bwd(
        qkv, grad_context_t, context_t, probs, inverse_total, key_rows, query_rows
    )
    grad_pos_key = lax.dot_general(
        pick, key_off.astype(bf), (((0,), (1,)), ((), ())), preferred_element_type=f32)
    grad_pos_query = lax.dot_general(
        pick, query_off.astype(bf), (((0,), (1,)), ((), ())), preferred_element_type=f32)
    low_pos_key = grad_pos_key.astype(bf)
    low_pos_query = grad_pos_query.astype(bf)
    d_w_query = tn(summed_low, d_query) + tn(rel, low_pos_query)
    d_w_key = tn(summed_low, d_key) + tn(rel, low_pos_key)
    d_w_value = tn(summed_low, d_value)
    d_b_query = jnp.sum(d_query.astype(f32), 0) + jnp.sum(grad_pos_query, 0)
    d_b_key = jnp.sum(d_key.astype(f32), 0) + jnp.sum(grad_pos_key, 0)
    d_b_value = jnp.sum(d_value.astype(f32), 0)
    w_q, w_k, w_v = w_qkv[:, :features], w_qkv[:, features : 2 * features], w_qkv[:, 2 * features :]
    d_rel = nt(low_pos_key, w_k) + nt(low_pos_query, w_q)
    grad_summed = nt(d_query, w_q) + nt(d_key, w_k) + nt(d_value, w_v) + grad_first
    whole = jnp.sum(grad_summed, 0)
    d_type_one = jnp.sum(jnp.where(second_part, grad_summed, 0.0), 0)
    tokens_grad = grad_summed.astype(bf).reshape(tokens.shape)

    share = lambda a: lax.psum_scatter(a.astype(bf), "fsdp", scatter_dimension=0, tiled=True)
    s_down, s_up, s_out = share(d_w_down), share(d_w_up), share(d_w_out)
    s_q, s_k, s_v, s_rel = share(d_w_query), share(d_w_key), share(d_w_value), share(d_rel)
    small = (d_b_query, d_b_key, d_b_value, d_b_out, d_first_gain, d_first_shift, d_b_up, d_b_down,
             d_second_gain, d_second_shift, whole - d_type_one, d_type_one)
    devices = lax.axis_size("fsdp")
    small = jnp.concatenate([a.reshape(devices, -1) for a in small], axis=1)
    small = lax.psum(small, ("rep", "fsdp"))
    small = lax.dynamic_index_in_dim(small, lax.axis_index("fsdp"), 0, keepdims=False)
    (d_b_query, d_b_key, d_b_value, d_b_out, d_first_gain, d_first_shift, d_b_up, d_b_down,
     d_second_gain, d_second_shift, d_type_zero, d_type_one) = [
        small[a:b] for a, b in zip(ends[:-1], ends[1:])]
    total = lambda a: lax.psum(a, "rep").astype(f32)
    return (
        layer_out, tokens_grad,
        total(s_q), d_b_query, total(s_k), d_b_key, total(s_v), d_b_value, total(s_out), d_b_out,
        d_first_gain, d_first_shift, total(s_up), d_b_up, total(s_down), d_b_down,
        d_second_gain, d_second_shift, total(s_rel), jnp.stack([d_type_zero, d_type_one]),
    )


def solution(mesh):
    seq = P(None, ("rep", "fsdp"), None, None)
    flat = P(None, ("rep", "fsdp"))
    mat, vec = P("fsdp", None), P("fsdp")
    weights = (mat, vec, mat, vec, mat, vec, mat, vec, vec, vec, mat, vec, mat, vec, vec, vec, mat,
               P(None, "fsdp"))
    return jax.shard_map(
        per_device,
        mesh=mesh,
        in_specs=(seq, flat, flat) + weights + (seq,),
        out_specs=(seq, seq) + weights,
        check_vma=False,
    )
```

```python
import math

import jax
import jax.numpy as jnp
import numpy as np
from jax import lax
from jax.experimental import pallas as pl
from jax.experimental.pallas import tpu as pltpu
from jax.sharding import PartitionSpec as P

BUCKETS = 256
MAX_POS = 512
NORM_EPS = 1e-07

HEAD_DIM=64
MASKED=-1e30
f32=jnp.float32; bf=jnp.bfloat16
BLK=128
LOG2E=math.log2(math.e)

def nn(a,b): return lax.dot_general(a,b,(((1,),(0,)),((),())),preferred_element_type=f32)
def nt(a,b): return lax.dot_general(a,b,(((1,),(1,)),((),())),preferred_element_type=f32)

def eye(rows, flip=False):
    r=lax.broadcasted_iota(jnp.int32,(rows,rows),0)
    c=lax.broadcasted_iota(jnp.int32,(rows,rows),1)
    return jnp.where((r+c==rows-1) if flip else (r==c),1.0,0.0).astype(bf)

def attn_fwd_kernel(len_ref,q_ref,k_ref,v_ref,pkr_ref,pq_ref,ctxT_ref,p_ref,linv_ref,c_scr,s_scr):
    S=q_ref.shape[0]
    nb=S//BLK
    W=S+BLK
    m=pl.program_id(1)
    length=len_ref[m]
    scale=LOG2E/math.sqrt(3*HEAD_DIM)
    q=q_ref[...]; k=k_ref[...]
    pq=pq_ref[...]
    vT=v_ref[...].T
    ident=eye(BLK)
    lane_s=lax.broadcasted_iota(jnp.int32,(S,2*HEAD_DIM),1)
    row_s=lax.broadcasted_iota(jnp.int32,(S,2*HEAD_DIM),0)
    lane_t=lax.broadcasted_iota(jnp.int32,(2*S,2*HEAD_DIM),1)
    bias=jnp.where(row_s<length,0.0,MASKED).astype(bf)
    zero=jnp.zeros((),bf)
    pos=lax.broadcasted_iota(jnp.int32,(1,S),1)
    for h in range(2):
        mine=(lane_s<HEAD_DIM) if h==0 else (lane_s>=HEAD_DIM)
        mine_t=(lane_t<HEAD_DIM) if h==0 else (lane_t>=HEAD_DIM)
        spare=HEAD_DIM if h==0 else 0
        qh=jnp.where(mine,q,zero)
        kb=jnp.where(mine,k,jnp.where(lane_s==spare,bias,zero))
        pqh=jnp.where(mine_t,pq,jnp.where(lane_t==spare,jnp.ones((),bf),zero))
        for b in range(nb):
            st=(nb-1-b)*BLK
            c=nt(qh[b*BLK:(b+1)*BLK],pkr_ref[st:st+W,:]).astype(bf)
            c_scr[b*BLK:(b+1)*BLK,:]=pltpu.roll(c,S+1,1,stride=1,stride_axis=0)[:,:S]
        top=None
        for b in range(nb):
            st=(nb-1-b)*BLK
            js=slice(b*BLK,(b+1)*BLK)
            d=nt(kb[js],pqh[st:st+W]).astype(bf)
            d=pltpu.roll(d,S+1,1,stride=1,stride_axis=0)[:,:S]
            lhs=jnp.concatenate([k[js],ident],axis=1)
            rhs=jnp.concatenate([qh,c_scr[:,js]],axis=1)
            s=nt(lhs,rhs)+d.astype(f32)
            s_scr[js,:]=s
            t=jnp.max(s,axis=0,keepdims=True)
            top=t if top is None else jnp.maximum(top,t)
        top=top*scale
        tot=None
        for b in range(nb):
            js=slice(b*BLK,(b+1)*BLK)
            p=jnp.exp2(s_scr[js,:]*scale-top).astype(bf)
            t=jnp.sum(p.astype(f32),axis=0,keepdims=True)
            tot=t if tot is None else tot+t
            p_ref[0,h,js,:]=p
        linv=jnp.where(pos<length,1.0/tot,0.0)
        linv_ref[0,0,h:h+1,:]=linv
        ctx=nn(vT[h*HEAD_DIM:(h+1)*HEAD_DIM,:],p_ref[0,h])*linv
        ctxT_ref[h*HEAD_DIM:(h+1)*HEAD_DIM,:]=ctx.astype(bf)

def attn_fwd(q,k,v,pkr,pq,lengths,heads):
    M=lengths.shape[0]; D=heads*HEAD_DIM
    S=pq.shape[0]//2
    NP=heads//2; L=2*HEAD_DIM
    grid=(NP,M)
    return pl.pallas_call(
        attn_fwd_kernel,
        grid_spec=pltpu.PrefetchScalarGridSpec(
            num_scalar_prefetch=1,grid=grid,
            in_specs=[
                pl.BlockSpec((S,L),lambda p,m,_:(m,p)),
                pl.BlockSpec((S,L),lambda p,m,_:(m,p)),
                pl.BlockSpec((S,L),lambda p,m,_:(m,p)),
                pl.BlockSpec((2*S,L),lambda p,m,_:(0,p)),
                pl.BlockSpec((2*S,L),lambda p,m,_:(0,p)),
            ],
            out_specs=[
                pl.BlockSpec((L,S),lambda p,m,_:(p,m)),
                pl.BlockSpec((1,2,S,S),lambda p,m,_:(m,p,0,0)),
                pl.BlockSpec((1,1,2,S),lambda p,m,_:(m,p,0,0)),
            ],
            scratch_shapes=[pltpu.VMEM((S,S),bf),pltpu.VMEM((S,S),f32)],
        ),
        out_shape=[jax.ShapeDtypeStruct((D,M*S),bf),jax.ShapeDtypeStruct((M,heads,S,S),bf),jax.ShapeDtypeStruct((M,NP,2,S),f32)],
        compiler_params=pltpu.CompilerParams(vmem_limit_bytes=40*1024*1024),
        cost_estimate=pl.CostEstimate(flops=int(2*M*heads*S*S*64*12),bytes_accessed=int(M*heads*S*S*2),transcendentals=M*heads*S*S),
    )(lengths,q,k,v,pkr,pq)

def attn_bwd_kernel(q_ref,k_ref,v_ref,dcT_ref,p_ref,linv_ref,pk_ref,pq_ref,dq_ref,dk_ref,dv_ref,ko_ref,qo_ref,ds_scr,p_scr,t_scr):
    S=q_ref.shape[0]
    nb=S//BLK
    W=S+BLK
    m=pl.program_id(1)
    scale=1.0/math.sqrt(3*HEAD_DIM)
    zero=jnp.zeros((),bf)
    ident=eye(BLK); flip=eye(BLK,True)
    q=q_ref[...]
    def reverse(x):
        return jnp.concatenate([nn(flip,x[(nb-1-b)*BLK:(nb-b)*BLK]).astype(bf) for b in range(nb)],axis=0)
    kr=reverse(k_ref[...]); vr=reverse(v_ref[...])
    qT=q.T; krT=kr.T
    lane_s=lax.broadcasted_iota(jnp.int32,(S,2*HEAD_DIM),1)
    lane_t=lax.broadcasted_iota(jnp.int32,(2*S,2*HEAD_DIM),1)
    pad=jnp.zeros((BLK,BLK),bf)
    @pl.when(m==0)
    def _():
        ko_ref[...]=jnp.zeros_like(ko_ref)
        qo_ref[...]=jnp.zeros_like(qo_ref)
    dq=[None]*nb; dk=[None]*nb; dv=None
    zrow=jnp.zeros((HEAD_DIM,S),bf)
    for h in range(2):
        hs=slice(h*HEAD_DIM,(h+1)*HEAD_DIM)
        mine=(lane_s<HEAD_DIM) if h==0 else (lane_s>=HEAD_DIM)
        mine_t=(lane_t<HEAD_DIM) if h==0 else (lane_t>=HEAD_DIM)
        qh=jnp.where(mine,q,zero); krh=jnp.where(mine,kr,zero)
        pkh=jnp.where(mine_t,pk_ref[...],zero); pqh=jnp.where(mine_t,pq_ref[...],zero)
        linv=linv_ref[0,0,h:h+1,:]
        dc=dcT_ref[hs,:].astype(f32)*linv
        dcl=dc.astype(bf); dcs=(dc*scale).astype(bf)
        def wide(x): return jnp.concatenate([x,zrow] if h==0 else [zrow,x],axis=0)
        t=nt(p_ref[0,h],wide(dcl))
        dv=t if dv is None else dv+t
        dcw=wide(dcs)
        delta=None
        for b in range(nb):
            js=slice(b*BLK,(b+1)*BLK)
            p=nn(flip,p_ref[0,h,(nb-1-b)*BLK:(nb-b)*BLK,:])
            t=p*nn(vr[js],dcw)
            p_scr[js,:]=p
            t_scr[js,:]=t
            t=jnp.sum(t,axis=0,keepdims=True)
            delta=t if delta is None else delta+t
        delta=delta*linv
        for b in range(nb):
            js=slice(b*BLK,(b+1)*BLK)
            ds=(t_scr[js,:]-p_scr[js,:]*delta).astype(bf)
            ds_scr[js,:]=ds
            far=pltpu.roll(jnp.concatenate([ds,pad],axis=1),0,1,stride=1,stride_axis=0)
            st=b*BLK
            t=nn(ds,qh)+nn(far,pqh[st:st+W])
            dk[b]=t if dk[b] is None else dk[b]+t
            qo_ref[hs,st:st+W]+=nn(krT[hs,js],far)
        for b in range(nb):
            js=slice(b*BLK,(b+1)*BLK)
            ds=nt(ident,ds_scr[:,js]).astype(bf)
            near=pltpu.roll(jnp.concatenate([ds,pad],axis=1),0,1,stride=1,stride_axis=0)
            st=b*BLK
            t=nn(ds,krh)+nn(near,pkh[st:st+W])
            dq[b]=t if dq[b] is None else dq[b]+t
            ko_ref[hs,st:st+W]+=nn(qT[hs,js],near)
    dv_ref[...]=dv.astype(bf)
    for b in range(nb):
        dq_ref[b*BLK:(b+1)*BLK,:]=dq[b].astype(bf)
        dk_ref[(nb-1-b)*BLK:(nb-b)*BLK,:]=nn(flip,dk[b].astype(bf)).astype(bf)

def attn_bwd(q,k,v,dcT,p,linv,pk,pq):
    M,heads,S,_=p.shape; D=heads*HEAD_DIM
    NP=heads//2; L=2*HEAD_DIM
    tok=lambda off: pl.BlockSpec((S,L),lambda p,m:(m,off+p))
    colT=pl.BlockSpec((L,S),lambda p,m:(p,m))
    tab=pl.BlockSpec((2*S,L),lambda p,m:(0,p))
    return pl.pallas_call(
        attn_bwd_kernel,
        grid=(NP,M),
        in_specs=[tok(0),tok(0),tok(0),colT,
            pl.BlockSpec((1,2,S,S),lambda p,m:(m,p,0,0)),
            pl.BlockSpec((1,1,2,S),lambda p,m:(m,p,0,0)),
            tab,tab],
        out_specs=[tok(0),tok(0),tok(0),pl.BlockSpec((L,2*S),lambda p,m:(p,0)),pl.BlockSpec((L,2*S),lambda p,m:(p,0))],
        out_shape=[jax.ShapeDtypeStruct((M*S,D),bf)]*3+[jax.ShapeDtypeStruct((D,2*S),f32)]*2,
        scratch_shapes=[pltpu.VMEM((S,S),bf),pltpu.VMEM((S,S),f32),pltpu.VMEM((S,S),f32)],
        compiler_params=pltpu.CompilerParams(vmem_limit_bytes=40*1024*1024),
        cost_estimate=pl.CostEstimate(flops=int(2*M*heads*S*S*64*24),bytes_accessed=int(M*heads*S*S*2),transcendentals=0),
    )(q,k,v,dcT,p,linv,pk,pq)


def bucket_index(offset_of):
    middle = BUCKETS // 2
    sign_of = np.sign(offset_of)
    magnitude = np.where(
        (offset_of < middle) & (offset_of > -middle), middle - 1, np.abs(offset_of)
    )
    log_pos = (
        np.ceil(np.log(magnitude / middle) / np.log((MAX_POS - 1) / middle) * (middle - 1)) + middle
    )
    bucket = np.where(magnitude <= middle, offset_of, log_pos * sign_of)
    return np.clip(bucket + BUCKETS, 0, 2 * BUCKETS - 1)


def pick_rows(offsets):
    return (bucket_index(offsets)[:, None] == np.arange(2 * BUCKETS)[None, :]).astype(np.float32)


def tn(a, b):
    return lax.dot_general(a, b, (((0,), (0,)), ((), ())), preferred_element_type=f32)


def normalize(values):
    centred = values - jnp.mean(values, -1, keepdims=True)
    inverse = lax.rsqrt(jnp.mean(centred * centred, -1, keepdims=True) + NORM_EPS)
    return centred * inverse, inverse


def normalize_back(grad, normed, inverse):
    return inverse * (
        grad
        - jnp.mean(grad, -1, keepdims=True)
        - normed * jnp.mean(grad * normed, -1, keepdims=True)
    )


def gelu_slope(values):
    cumulative = 0.5 * (1.0 + lax.erf(values * (1.0 / math.sqrt(2.0))))
    density = jnp.exp(-0.5 * values * values) * (1.0 / math.sqrt(2.0 * math.pi))
    return cumulative + values * density


TILE = 16


def swap_core(a):
    n = lax.axis_size("fsdp")
    return lax.ppermute(a, "fsdp", [(i, i ^ 1) for i in range(n)])


def swap_line(a):
    n = lax.axis_size("fsdp")
    groups = [list(range(c, n, 2)) for c in range(2)]
    return lax.all_to_all(a, "fsdp", 0, 0, tiled=True, axis_index_groups=groups)


def along_line(a, step):
    n = lax.axis_size("fsdp")
    return lax.ppermute(a, "fsdp", [(i, i + 2 * step) for i in range(n) if 0 <= i + 2 * step < n])


def swap_rep(a):
    return lax.all_to_all(a, "rep", 0, 0, tiled=True)


def flip_rep(a, bit):
    return lax.ppermute(a, "rep", [(i, i ^ bit) for i in range(lax.axis_size("rep"))])


def spread(a, copies):
    return jnp.broadcast_to(a[None], (copies,) + a.shape)


def gather_rep(a):
    reps = lax.axis_size("rep")
    bits = [1 << k for k in range(reps.bit_length() - 1)]
    width = a.shape[-1] // len(bits)
    me = lax.axis_index("rep")
    shares = []
    for k in range(len(bits)):
        share = a[None, ..., k * width : (k + 1) * width]
        order = bits[k:] + bits[:k]
        for bit in order:
            other = flip_rep(share, bit)
            high = (me // bit) % 2 == 1
            share = jnp.concatenate([jnp.where(high, other, share), jnp.where(high, share, other)])
        at = np.zeros(reps, np.int32)
        for place in range(reps):
            rep = sum(bit for i, bit in enumerate(order) if (place >> i) & 1)
            at[rep] = place
        shares.append(jnp.stack([share[int(p)] for p in at]))
    return jnp.concatenate(shares, axis=-1)


def gather_parts(mine, shard, *others):
    places = lax.axis_size("fsdp") // 2
    place = lax.axis_index("fsdp") // 2
    steps = [k for d in range(1, places) for k in (d, -d)]
    seen = {-k: along_line(mine, k) for k in steps}
    line = jnp.stack([seen[k] for k in range(1 - places, places) if k])
    line = lax.dynamic_slice_in_dim(line, places - 1 - place, places - 1, 0)
    line, *others = lax.optimization_barrier((line, *others))
    every = gather_rep(line)
    at = jnp.arange(places)[None, :, None, None]
    before = jnp.pad(every, ((0, 0), (0, 1), (0, 0), (0, 0)))
    behind = jnp.pad(every, ((0, 0), (1, 0), (0, 0), (0, 0)))
    every = jnp.where(at == place, shard[:, None], jnp.where(at < place, before, behind))
    other = swap_core(every)
    first = lax.axis_index("fsdp") % 2 == 0
    return jnp.stack([jnp.where(first, every, other), jnp.where(first, other, every)], axis=2), others


def reduce_core(values):
    core = lax.axis_index("fsdp") % 2
    keep = lax.dynamic_index_in_dim(values, core, 2, keepdims=False)
    give = lax.dynamic_index_in_dim(values, 1 - core, 2, keepdims=False)
    return (keep.astype(f32) + swap_core(give).astype(f32)).astype(bf)


def summed_over(a):
    return jnp.sum(a.astype(f32), 0).astype(bf)


def pad_tail(a, rows, columns):
    return jnp.pad(a, [(0, 0)] * (a.ndim - 2) + [(0, rows - a.shape[-2]), (0, columns - a.shape[-1])])


def per_device(
    tokens, lengths, boundary,
    w_query, b_query, w_key, b_key, w_value, b_value, w_out, b_out,
    first_gain, first_shift, w_up, b_up, w_down, b_down,
    second_gain, second_shift, rel_table, type_table, out_grad,
):
    micros, seqs, seq_len, features = tokens.shape
    rows = micros * seqs * seq_len
    heads = features // HEAD_DIM
    fs, reps = lax.axis_size("fsdp"), lax.axis_size("rep")
    places = fs // 2
    cut = w_query.shape[0]
    unit = 4 * cut // reps
    table_cut = rel_table.shape[0] // reps
    up_parts = w_up.shape[1] // features
    vectors = jnp.stack([b_query, b_key, b_value, b_out, first_gain, first_shift, b_down, second_gain,
                         second_shift, type_table[0], type_table[1]] + [b_up[k * cut : (k + 1) * cut] for k in range(up_parts)])
    vector_count = vectors.shape[0]
    vector_rows = -(-vector_count // TILE) * TILE
    vectors = pad_tail(vectors, vector_rows, features)
    shard = jnp.concatenate([
        jnp.stack([w_query, w_key, w_value, w_out]).reshape(reps, unit, features),
        rel_table.reshape(reps, table_cut, features),
        spread(vectors, reps)], axis=1)
    mine = lax.dynamic_index_in_dim(shard, lax.axis_index("rep"), 0, keepdims=False)
    first, (w_up, w_down) = gather_parts(mine, shard, w_up, w_down)
    w_u = lax.all_gather(w_up, "fsdp", axis=0, tiled=True)
    w_d = lax.all_gather(w_down, "fsdp", axis=0, tiled=True)
    four = first[:, :, :, :unit].reshape(4, reps // 4, fs, unit, features).transpose(0, 2, 1, 3, 4)
    four = four.reshape(4, features, features)
    rel = first[:, :, :, unit : unit + table_cut].transpose(1, 2, 0, 3, 4).reshape(-1, features)
    wide = first[0, :, :, unit + table_cut : unit + table_cut + vector_count, :cut].reshape(fs, vector_count, cut)
    wide = wide.transpose(1, 0, 2).astype(f32)
    v_up = wide[vector_count - up_parts :].transpose(1, 0, 2).reshape(-1)
    wide = wide.reshape(vector_count, features)
    (v_query, v_key, v_value, v_out, g_first, s_first, v_down, g_second, s_second,
     type_zero, type_one) = [wide[k] for k in range(vector_count - up_parts)]
    w_q, w_k, w_v, w_o = [four[k] for k in range(4)]

    offsets = np.clip(np.arange(2 * seq_len) - (seq_len - 1), 1 - seq_len, seq_len - 1)
    pick = jnp.asarray(pick_rows(offsets), bf)
    pick_back = jnp.asarray(pick_rows(-offsets), bf)

    positions = jnp.arange(seq_len)
    second_part = (positions[None, None, :] >= boundary[:, :, None]).reshape(rows, 1)
    summed = tokens.reshape(rows, features).astype(f32) + jnp.where(second_part, type_one, type_zero)
    summed_low = summed.astype(bf)
    queries = (nn(summed_low, w_q) + v_query).astype(bf)
    keys = (nn(summed_low, w_k) + v_key).astype(bf)
    values = (nn(summed_low, w_v) + v_value).astype(bf)
    pos_query = (nn(rel, w_q) + v_query).astype(bf)
    pos_key = (nn(rel, w_k) + v_key).astype(bf)
    key_rows = nn(pick, pos_key).astype(bf)
    key_rows_back = nn(pick_back, pos_key).astype(bf)
    query_rows = nn(pick, pos_query).astype(bf)
    flat_lengths = lengths.reshape(-1)
    context_t, probs, inverse_total = attn_fwd(queries, keys, values, key_rows_back, query_rows, flat_lengths, heads)
    attended = tn(context_t, w_o) + v_out
    first_normed, first_inverse = normalize(summed + attended)
    hidden = first_normed * g_first + s_first
    hidden_low = hidden.astype(bf)
    raised = nn(hidden_low, w_u) + v_up
    active = jax.nn.gelu(raised, approximate=False).astype(bf)
    second_normed, second_inverse = normalize(hidden + nn(active, w_d) + v_down)
    layer_out = (second_normed * g_second + s_second).astype(bf).reshape(tokens.shape)

    grad_output = out_grad.reshape(rows, features).astype(f32)
    d_second_gain = jnp.sum(grad_output * second_normed, 0)
    d_second_shift = jnp.sum(grad_output, 0)
    grad_mixed = normalize_back(grad_output * g_second, second_normed, second_inverse)
    grad_ffn = grad_mixed.astype(bf)
    d_w_down = tn(active, grad_ffn)
    d_b_down = jnp.sum(grad_ffn.astype(f32), 0)
    grad_raised = (nt(grad_ffn, w_d) * gelu_slope(raised)).astype(bf)
    d_w_up = tn(hidden_low, grad_raised)
    d_b_up = jnp.sum(grad_raised.astype(f32), 0)
    share = lambda a: lax.psum_scatter(a, "fsdp", scatter_dimension=0, tiled=True)
    s_down = share(d_w_down.astype(bf))
    s_up = share(d_w_up.astype(bf))
    grad_hidden = nt(grad_raised, w_u) + grad_mixed
    d_first_gain = jnp.sum(grad_hidden * first_normed, 0)
    d_first_shift = jnp.sum(grad_hidden, 0)
    grad_first = normalize_back(grad_hidden * g_first, first_normed, first_inverse)
    grad_attended = grad_first.astype(bf)
    d_w_out = nn(context_t, grad_attended)
    d_b_out = jnp.sum(grad_attended.astype(f32), 0)
    grad_context_t = nt(w_o, grad_attended).astype(bf)
    d_query, d_key, d_value, key_off, query_off = attn_bwd(
        queries, keys, values, grad_context_t, probs, inverse_total, key_rows, query_rows
    )
    d_query, d_key, d_value, key_off, query_off, s_down, s_up = lax.optimization_barrier(
        (d_query, d_key, d_value, key_off, query_off, s_down, s_up))
    s_down, s_up = lax.psum((s_down, s_up), "rep")
    grad_pos_key = lax.dot_general(
        pick, key_off.astype(bf), (((0,), (1,)), ((), ())), preferred_element_type=f32)
    grad_pos_query = lax.dot_general(
        pick, query_off.astype(bf), (((0,), (1,)), ((), ())), preferred_element_type=f32)
    low_pos_key = grad_pos_key.astype(bf)
    low_pos_query = grad_pos_query.astype(bf)
    d_w_query = tn(summed_low, d_query) + tn(rel, low_pos_query)
    d_w_key = tn(summed_low, d_key) + tn(rel, low_pos_key)
    d_w_value = tn(summed_low, d_value)
    d_b_query = jnp.sum(d_query.astype(f32), 0) + jnp.sum(grad_pos_query, 0)
    d_b_key = jnp.sum(d_key.astype(f32), 0) + jnp.sum(grad_pos_key, 0)
    d_b_value = jnp.sum(d_value.astype(f32), 0)
    d_rel = nt(low_pos_key, w_k) + nt(low_pos_query, w_q)
    grad_summed = nt(d_query, w_q) + nt(d_key, w_k) + nt(d_value, w_v) + grad_first
    whole = jnp.sum(grad_summed, 0)
    d_type_one = jnp.sum(jnp.where(second_part, grad_summed, 0.0), 0)
    tokens_grad = grad_summed.astype(bf).reshape(tokens.shape)

    small = jnp.stack([d_b_query, d_b_key, d_b_value, d_b_out, d_first_gain, d_first_shift, d_b_down,
                       d_second_gain, d_second_shift, whole - d_type_one, d_type_one])
    small = small.astype(bf).reshape(-1, fs, cut).transpose(1, 0, 2)
    small = jnp.concatenate([small, d_b_up.astype(bf).reshape(fs, up_parts, cut)], axis=1)
    small = pad_tail(small.reshape(places, 2, vector_count, cut), vector_rows, features)
    four = jnp.stack([a.astype(bf) for a in (d_w_query, d_w_key, d_w_value, d_w_out)])
    four = four.reshape(4, places, 2, reps // 4, unit, features).transpose(0, 3, 1, 2, 4, 5)
    last = jnp.concatenate([
        four.reshape(reps, places, 2, unit, features),
        d_rel.astype(bf).reshape(places, 2, reps, table_cut, features).transpose(2, 0, 1, 3, 4),
        spread(small, reps)], axis=3)
    last = summed_over(swap_rep(reduce_core(last)))
    last, s_down, s_up = lax.optimization_barrier((last, s_down, s_up))
    last = summed_over(swap_line(last))
    small = last[unit + table_cut :, :cut].astype(f32)
    both = swap_rep(spread(last[: unit + table_cut], reps)).astype(f32)
    four = both[:, :unit].reshape(4, cut, features)
    s_q, s_k, s_v, s_o = four[0], four[1], four[2], four[3]
    s_rel = both[:, unit:].reshape(-1, features)
    (d_b_query, d_b_key, d_b_value, d_b_out, d_first_gain, d_first_shift, d_b_down,
     d_second_gain, d_second_shift, d_type_zero, d_type_one) = [
        small[k] for k in range(vector_count - up_parts)]
    d_b_up = small[vector_count - up_parts : vector_count].reshape(-1)
    s_down, s_up = s_down.astype(f32), s_up.astype(f32)
    return (
        layer_out, tokens_grad,
        s_q, d_b_query, s_k, d_b_key, s_v, d_b_value, s_o, d_b_out,
        d_first_gain, d_first_shift, s_up, d_b_up, s_down, d_b_down,
        d_second_gain, d_second_shift, s_rel, jnp.stack([d_type_zero, d_type_one]),
    )


def solution(mesh):
    seq = P(None, ("rep", "fsdp"), None, None)
    flat = P(None, ("rep", "fsdp"))
    mat, vec = P("fsdp", None), P("fsdp")
    weights = (mat, vec, mat, vec, mat, vec, mat, vec, vec, vec, mat, vec, mat, vec, vec, vec, mat,
               P(None, "fsdp"))
    return jax.shard_map(
        per_device,
        mesh=mesh,
        in_specs=(seq, flat, flat) + weights + (seq,),
        out_specs=(seq, seq) + weights,
        check_vma=False,
    )
```

```python
import math

import jax
import jax.numpy as jnp
import numpy as np
from jax import lax
from jax.experimental import pallas as pl
from jax.experimental.pallas import tpu as pltpu
from jax.sharding import PartitionSpec as P

BUCKETS = 256
MAX_POS = 512
NORM_EPS = 1e-07
VMEM_LIMIT = 62 * 1024 * 1024

HEAD_DIM=64
MASKED=-1e30
f32=jnp.float32; bf=jnp.bfloat16
BLK=128
LOG2E=math.log2(math.e)

def nn(a,b): return lax.dot_general(a,b,(((1,),(0,)),((),())),preferred_element_type=f32)
def nt(a,b): return lax.dot_general(a,b,(((1,),(1,)),((),())),preferred_element_type=f32)

def eye(rows, flip=False):
    r=lax.broadcasted_iota(jnp.int32,(rows,rows),0)
    c=lax.broadcasted_iota(jnp.int32,(rows,rows),1)
    return jnp.where((r+c==rows-1) if flip else (r==c),1.0,0.0).astype(bf)

def attn_fwd_kernel(len_ref,q_ref,k_ref,v_ref,pkrT_ref,pqT_ref,ctxT_ref,p_ref,linv_ref,c_scr,s_scr):
    S=q_ref.shape[0]
    nb=S//BLK
    W=S+BLK
    m=pl.program_id(1)
    length=len_ref[m]
    scale=LOG2E/math.sqrt(3*HEAD_DIM)
    q=q_ref[...]; k=k_ref[...]
    pqT=pqT_ref[...]
    vT=v_ref[...].T; qT=q.T
    row_h=lax.broadcasted_iota(jnp.int32,(2*HEAD_DIM,S),0)
    lane_s=lax.broadcasted_iota(jnp.int32,(S,2*HEAD_DIM),1)
    row_s=lax.broadcasted_iota(jnp.int32,(S,2*HEAD_DIM),0)
    row_t=lax.broadcasted_iota(jnp.int32,(2*HEAD_DIM,2*S),0)
    bias=jnp.where(row_s<length,0.0,MASKED).astype(bf)
    zero=jnp.zeros((),bf)
    pos=lax.broadcasted_iota(jnp.int32,(1,S),1)
    for h in range(2):
        mine=(lane_s<HEAD_DIM) if h==0 else (lane_s>=HEAD_DIM)
        spare=HEAD_DIM if h==0 else 0
        qh=jnp.where(mine,q,zero)
        kb=jnp.where(mine,k,jnp.where(lane_s==spare,bias,zero))
        pqh=jnp.where(row_t==spare,jnp.ones((),bf),pqT)
        qTh=jnp.where((row_h<HEAD_DIM) if h==0 else (row_h>=HEAD_DIM),qT,zero)
        for b in range(nb):
            st=(nb-1-b)*BLK
            c=nn(qh[b*BLK:(b+1)*BLK],pkrT_ref[:,st:st+W]).astype(bf)
            c_scr[h,b*BLK:(b+1)*BLK,:]=pltpu.roll(c,S+1,1,stride=1,stride_axis=0)[:,:S]
        top=None
        for b in range(nb):
            st=(nb-1-b)*BLK
            js=slice(b*BLK,(b+1)*BLK)
            d=nn(kb[js],pqh[:,st:st+W]).astype(bf)
            d=pltpu.roll(d,S+1,1,stride=1,stride_axis=0)[:,:S]
            s=nn(k[js],qTh)+(c_scr[h,:,js].T.astype(f32)+d.astype(f32))
            s_scr[h,js,:]=s
            t=jnp.max(s,axis=0,keepdims=True)
            top=t if top is None else jnp.maximum(top,t)
        top=top*scale
        tot=None
        for b in range(nb):
            js=slice(b*BLK,(b+1)*BLK)
            p=jnp.exp2(s_scr[h,js,:]*scale-top).astype(bf)
            t=jnp.sum(p.astype(f32),axis=0,keepdims=True)
            tot=t if tot is None else tot+t
            p_ref[0,h,js,:]=p
        linv=jnp.where(pos<length,1.0/tot,0.0)
        linv_ref[0,0,h:h+1,:]=linv
        ctx=nn(vT[h*HEAD_DIM:(h+1)*HEAD_DIM,:],p_ref[0,h])*linv
        ctxT_ref[h*HEAD_DIM:(h+1)*HEAD_DIM,:]=ctx.astype(bf)

def attn_fwd(q,k,v,pkr,pq,lengths,heads):
    M=lengths.shape[0]; D=heads*HEAD_DIM
    S=pq.shape[1]//2
    NP=heads//2; L=2*HEAD_DIM
    grid=(NP,M)
    return pl.pallas_call(
        attn_fwd_kernel,
        grid_spec=pltpu.PrefetchScalarGridSpec(
            num_scalar_prefetch=1,grid=grid,
            in_specs=[
                pl.BlockSpec((S,L),lambda p,m,_:(m,p)),
                pl.BlockSpec((S,L),lambda p,m,_:(m,p)),
                pl.BlockSpec((S,L),lambda p,m,_:(m,p)),
                pl.BlockSpec((L,2*S),lambda p,m,_:(p,0)),
                pl.BlockSpec((L,2*S),lambda p,m,_:(p,0)),
            ],
            out_specs=[
                pl.BlockSpec((L,S),lambda p,m,_:(p,m)),
                pl.BlockSpec((1,2,S,S),lambda p,m,_:(m,p,0,0)),
                pl.BlockSpec((1,1,2,S),lambda p,m,_:(m,p,0,0)),
            ],
            scratch_shapes=[pltpu.VMEM((2,S,S),bf),pltpu.VMEM((2,S,S),f32)],
        ),
        out_shape=[jax.ShapeDtypeStruct((D,M*S),bf),jax.ShapeDtypeStruct((M,heads,S,S),bf),jax.ShapeDtypeStruct((M,NP,2,S),f32)],
        compiler_params=pltpu.CompilerParams(vmem_limit_bytes=VMEM_LIMIT),
        cost_estimate=pl.CostEstimate(flops=int(2*M*heads*S*S*64*12),bytes_accessed=int(M*heads*S*S*2),transcendentals=M*heads*S*S),
    )(lengths,q,k,v,pkr,pq)

def attn_bwd_kernel(q_ref,k_ref,v_ref,dcT_ref,p_ref,linv_ref,pk_ref,pq_ref,dq_ref,dk_ref,dv_ref,ko_out,qo_out,ds_scr,p_scr,t_scr,ko_ref,qo_ref):
    S=q_ref.shape[0]
    nb=S//BLK
    W=S+BLK
    m=pl.program_id(1)
    scale=1.0/math.sqrt(3*HEAD_DIM)
    zero=jnp.zeros((),bf)
    flip=eye(BLK,True)
    q=q_ref[...]
    def reverse(x):
        return jnp.concatenate([nn(flip,x[(nb-1-b)*BLK:(nb-b)*BLK]).astype(bf) for b in range(nb)],axis=0)
    kr=reverse(k_ref[...]); vr=reverse(v_ref[...])
    qT=q.T; krT=kr.T
    lane_s=lax.broadcasted_iota(jnp.int32,(S,2*HEAD_DIM),1)
    lane_t=lax.broadcasted_iota(jnp.int32,(2*S,2*HEAD_DIM),1)
    pad=jnp.zeros((BLK,BLK),bf)
    @pl.when(m==0)
    def _():
        ko_ref[...]=jnp.zeros_like(ko_ref)
        qo_ref[...]=jnp.zeros_like(qo_ref)
    dq=[None]*nb; dk=[None]*nb; dv=None
    zrow=jnp.zeros((HEAD_DIM,S),bf)
    for h in range(2):
        hs=slice(h*HEAD_DIM,(h+1)*HEAD_DIM)
        mine=(lane_s<HEAD_DIM) if h==0 else (lane_s>=HEAD_DIM)
        mine_t=(lane_t<HEAD_DIM) if h==0 else (lane_t>=HEAD_DIM)
        qh=jnp.where(mine,q,zero); krh=jnp.where(mine,kr,zero)
        pkh=jnp.where(mine_t,pk_ref[...],zero); pqh=jnp.where(mine_t,pq_ref[...],zero)
        linv=linv_ref[0,0,h:h+1,:]
        dc=dcT_ref[hs,:].astype(f32)*linv
        dcl=dc.astype(bf); dcs=(dc*scale).astype(bf)
        def wide(x): return jnp.concatenate([x,zrow] if h==0 else [zrow,x],axis=0)
        t=nt(p_ref[0,h],wide(dcl))
        dv=t if dv is None else dv+t
        dcw=wide(dcs)
        delta=None
        for b in range(nb):
            js=slice(b*BLK,(b+1)*BLK)
            p=nn(flip,p_ref[0,h,(nb-1-b)*BLK:(nb-b)*BLK,:])
            t=p*nn(vr[js],dcw)
            p_scr[h,js,:]=p
            t_scr[h,js,:]=t
            t=jnp.sum(t,axis=0,keepdims=True)
            delta=t if delta is None else delta+t
        delta=delta*linv
        for b in range(nb):
            js=slice(b*BLK,(b+1)*BLK)
            ds=(t_scr[h,js,:]-p_scr[h,js,:]*delta).astype(bf)
            ds_scr[h,js,:]=ds
            far=pltpu.roll(jnp.concatenate([ds,pad],axis=1),0,1,stride=1,stride_axis=0)
            st=b*BLK
            t=nn(ds,qh)+nn(far,pqh[st:st+W])
            dk[b]=t if dk[b] is None else dk[b]+t
            qo_ref[hs,st:st+W]+=nn(krT[hs,js],far)
        for b in range(nb):
            js=slice(b*BLK,(b+1)*BLK)
            ds=ds_scr[h,:,js].T
            near=pltpu.roll(jnp.concatenate([ds,pad],axis=1),0,1,stride=1,stride_axis=0)
            st=b*BLK
            t=nn(ds,krh)+nn(near,pkh[st:st+W])
            dq[b]=t if dq[b] is None else dq[b]+t
            ko_ref[hs,st:st+W]+=nn(qT[hs,js],near)
    @pl.when(m==pl.num_programs(1)-1)
    def _():
        ko_out[...]=ko_ref[...].astype(bf)
        qo_out[...]=qo_ref[...].astype(bf)
    dv_ref[...]=dv.astype(bf)
    for b in range(nb):
        dq_ref[b*BLK:(b+1)*BLK,:]=dq[b].astype(bf)
        dk_ref[(nb-1-b)*BLK:(nb-b)*BLK,:]=nn(flip,dk[b].astype(bf)).astype(bf)

def attn_bwd(q,k,v,dcT,p,linv,pk,pq):
    M,heads,S,_=p.shape; D=heads*HEAD_DIM
    NP=heads//2; L=2*HEAD_DIM
    tok=lambda off: pl.BlockSpec((S,L),lambda p,m:(m,off+p))
    colT=pl.BlockSpec((L,S),lambda p,m:(p,m))
    tab=pl.BlockSpec((2*S,L),lambda p,m:(0,p))
    return pl.pallas_call(
        attn_bwd_kernel,
        grid=(NP,M),
        in_specs=[tok(0),tok(0),tok(0),colT,
            pl.BlockSpec((1,2,S,S),lambda p,m:(m,p,0,0)),
            pl.BlockSpec((1,1,2,S),lambda p,m:(m,p,0,0)),
            tab,tab],
        out_specs=[tok(0),tok(0),tok(0),pl.BlockSpec((L,2*S),lambda p,m:(p,0)),pl.BlockSpec((L,2*S),lambda p,m:(p,0))],
        out_shape=[jax.ShapeDtypeStruct((M*S,D),bf)]*3+[jax.ShapeDtypeStruct((D,2*S),bf)]*2,
        scratch_shapes=[pltpu.VMEM((2,S,S),bf),pltpu.VMEM((2,S,S),f32),pltpu.VMEM((2,S,S),f32),pltpu.VMEM((L,2*S),f32),pltpu.VMEM((L,2*S),f32)],
        compiler_params=pltpu.CompilerParams(vmem_limit_bytes=VMEM_LIMIT),
        cost_estimate=pl.CostEstimate(flops=int(2*M*heads*S*S*64*24),bytes_accessed=int(M*heads*S*S*2),transcendentals=0),
    )(q,k,v,dcT,p,linv,pk,pq)


def bucket_index(offset_of):
    middle = BUCKETS // 2
    sign_of = np.sign(offset_of)
    magnitude = np.where(
        (offset_of < middle) & (offset_of > -middle), middle - 1, np.abs(offset_of)
    )
    log_pos = (
        np.ceil(np.log(magnitude / middle) / np.log((MAX_POS - 1) / middle) * (middle - 1)) + middle
    )
    bucket = np.where(magnitude <= middle, offset_of, log_pos * sign_of)
    return np.clip(bucket + BUCKETS, 0, 2 * BUCKETS - 1)


def pick_rows(offsets):
    return (bucket_index(offsets)[:, None] == np.arange(2 * BUCKETS)[None, :]).astype(np.float32)


def tn(a, b):
    return lax.dot_general(a, b, (((0,), (0,)), ((), ())), preferred_element_type=f32)

COLUMNS = 256


def second_rows(bound_ref, rows, seq_len):
    at = lax.broadcasted_iota(jnp.int32, (rows, 1), 0)
    second = at < 0
    for m in range(rows // seq_len):
        second = second | ((at >= m * seq_len + bound_ref[m]) & (at < (m + 1) * seq_len))
    return second


def project_kernel(
    bound_ref, tokens_ref, w_q_ref, w_k_ref, w_v_ref, rel_ref, pick_ref, pick_t_ref, pick_back_t_ref, vec_ref,
    type_ref, q_ref, k_ref, v_ref, key_ref, query_ref, key_back_ref, query_t_ref, low_ref, *, seq_len,
):
    rows = tokens_ref.shape[0]

    @pl.when(pl.program_id(0) == 0)
    def _():
        second = second_rows(bound_ref, rows, seq_len)
        low_ref[...] = (
            tokens_ref[...].astype(f32) + jnp.where(second, type_ref[1:2, :], type_ref[0:1, :])
        ).astype(bf)

    low = low_ref[...]
    rel = rel_ref[...].reshape(-1, tokens_ref.shape[1])
    features = tokens_ref.shape[1]
    w_q, w_k, w_v = [r[...].reshape(features, -1) for r in (w_q_ref, w_k_ref, w_v_ref)]
    b_q, b_k = vec_ref[0:1, :], vec_ref[1:2, :]
    q_ref[...] = (nn(low, w_q) + b_q).astype(bf)
    k_ref[...] = (nn(low, w_k) + b_k).astype(bf)
    v_ref[...] = (nn(low, w_v) + vec_ref[2:3, :]).astype(bf)
    pos_query = (nn(rel, w_q) + b_q).astype(bf)
    pos_key = (nn(rel, w_k) + b_k).astype(bf)
    query_ref[...] = nn(pick_ref[...], pos_query).astype(bf)
    key_ref[...] = nn(pick_ref[...], pos_key).astype(bf)
    key_back_ref[...] = tn(pos_key, pick_back_t_ref[...]).astype(bf)
    query_t_ref[...] = tn(pos_query, pick_t_ref[...]).astype(bf)


def weight_view(view, g, columns):
    lead, rows = view[1], view[2]
    return pl.BlockSpec(lead + (1, rows, columns), lambda i, *_: (0, 0, g, 0, i if columns == COLUMNS else 0),
                        pipeline_mode=None if columns == COLUMNS else pl.Buffered(1))


def table_view(view):
    return pl.BlockSpec(view[4], lambda i, *_: view[5], pipeline_mode=pl.Buffered(1))


def project(boundary, tokens, view, pick, pick_t, pick_back_t, vec, types, seq_len):
    total, features = tokens.shape
    four, table = view[0], view[3]
    table_rows = pick.shape[1]
    whole = lambda a: pl.BlockSpec(a.shape, lambda i, _: (0,) * a.ndim, pipeline_mode=pl.Buffered(1))
    weight = lambda g: weight_view(view, g, COLUMNS)
    columns = lambda rows: pl.BlockSpec((rows, COLUMNS), lambda i, _: (0, i))
    shape = jax.ShapeDtypeStruct
    offsets = pick.shape[0]
    return pl.pallas_call(
        lambda *refs: project_kernel(*refs, seq_len=seq_len),
        grid_spec=pltpu.PrefetchScalarGridSpec(
            num_scalar_prefetch=1,
            grid=(features // COLUMNS,),
            in_specs=[whole(tokens), weight(0), weight(1), weight(2), table_view(view), whole(pick),
                      whole(pick_t), whole(pick_back_t), columns(vec.shape[0]), whole(types)],
            out_specs=[columns(total)] * 3 + [columns(offsets)] * 2
            + [pl.BlockSpec((COLUMNS, offsets), lambda i, _: (i, 0))] * 2
            + [pl.BlockSpec((total, features), lambda i, _: (0, 0))],
        ),
        out_shape=[shape((total, features), bf)] * 3 + [shape((offsets, features), bf)] * 2
        + [shape((features, offsets), bf)] * 2
        + [shape((total, features), bf)],
        compiler_params=pltpu.CompilerParams(vmem_limit_bytes=VMEM_LIMIT),
        cost_estimate=pl.CostEstimate(
            flops=2 * features * features * (3 * total + 2 * table_rows) + 6 * offsets * features * table_rows,
            bytes_accessed=2 * features * (3 * features + 5 * total + 3 * offsets), transcendentals=0),
    )(boundary, tokens, four, four, four, table, pick, pick_t, pick_back_t, vec, types)


def unproject_kernel(
    bound_ref, core_ref, low_ref, dq_ref, dk_ref, dv_ref, key_off_ref, query_off_ref, w_q_ref, w_k_ref, w_v_ref,
    rel_ref, pick_t_ref, grad_first_ref, context_ref, grad_att_ref, sums_ref, sum_up_ref,
    *refs, seq_len, direct,
):
    if direct:
        keep_ref, give_ref, grad_ref, sum_ref, rel_sum_ref, small_ref = refs
    else:
        dw_ref, drel_ref, small_ref, grad_ref, sum_ref, rel_sum_ref = refs
    step = pl.program_id(0)
    rows, features = low_ref.shape
    first = core_ref[0] == 0

    @pl.when(step == 0)
    def _():
        sum_ref[...] = grad_first_ref[...]
        rel_sum_ref[...] = jnp.zeros_like(rel_sum_ref)
        small_ref[...] = jnp.zeros_like(small_ref)

    low, rel = low_ref[...], rel_ref[...].reshape(-1, features)
    w_q, w_k, w_v = [r[...].reshape(features, -1) for r in (w_q_ref, w_k_ref, w_v_ref)]
    dq, dk, dv = dq_ref[...], dk_ref[...], dv_ref[...]
    columns = pl.ds(pl.multiple_of(step * COLUMNS, COLUMNS), COLUMNS)

    def put(at, rows_at, values):
        if direct:
            _, places, part, _ = keep_ref.shape
            values = values.astype(bf).reshape(places, 2, -1, values.shape[-1])
            keep_ref[at, :, rows_at, columns] = jnp.where(first, values[:, 0], values[:, 1])
            give_ref[at, :, rows_at, columns] = jnp.where(first, values[:, 1], values[:, 0])
        else:
            dw_ref[at] = values.astype(bf)

    unit = direct
    pos_query = nt(pick_t_ref[...], query_off_ref[...])
    pos_key = nt(pick_t_ref[...], key_off_ref[...])
    low_query, low_key = pos_query.astype(bf), pos_key.astype(bf)
    put(0, slice(0, unit), tn(low, dq) + tn(rel, low_query))
    put(1, slice(0, unit), tn(low, dk) + tn(rel, low_key))
    put(2, slice(0, unit), tn(low, dv))
    put(3, slice(0, unit), nn(context_ref[...], grad_att_ref[...]))
    total = lambda a: jnp.sum(a.astype(f32), 0, keepdims=True)
    small_ref[0:1, columns] = total(dq) + total(pos_query)
    small_ref[1:2, columns] = total(dk) + total(pos_key)
    small_ref[2:3, columns] = total(dv)
    sum_ref[...] += nt(dq, w_q) + nt(dk, w_k) + nt(dv, w_v)
    rel_sum_ref[...] += nt(low_key, w_k) + nt(low_query, w_q)

    @pl.when(step == pl.num_programs(0) - 1)
    def _():
        values = sum_ref[...]
        grad_ref[...] = values.astype(bf)
        second = second_rows(bound_ref, rows, seq_len)
        for at, k in ((3, 5), (4, 3), (5, 4), (6, 2), (7, 0), (8, 1)):
            small_ref[at : at + 1, :] = sums_ref[k : k + 1, :]
        small_ref[9:10, :] = total(jnp.where(second, 0.0, values))
        small_ref[10:11, :] = total(jnp.where(second, values, 0.0))
        for k in range(sum_up_ref.shape[1] // features):
            small_ref[11 + k : 12 + k, :] = sum_up_ref[:, k * features : (k + 1) * features]
        if direct:
            reps, places, part, _ = keep_ref.shape
            table = rel_sum_ref[...].astype(bf).reshape(places, 2, reps, -1, features)
            small = small_ref[...].astype(bf)
            end = unit + table.shape[3]
            for r in range(reps):
                keep_ref[r, :, unit:end, :] = jnp.where(first, table[:, 0, r], table[:, 1, r])
                give_ref[r, :, unit:end, :] = jnp.where(first, table[:, 1, r], table[:, 0, r])
                for z in range(places):
                    keep_ref[r, z, end:part, :] = small
                    give_ref[r, z, end:part, :] = small
        else:
            drel_ref[...] = rel_sum_ref[...].astype(bf)


def unproject(boundary, core, low, dq, dk, dv, key_off, query_off, view, pick_t, grad_first, context_t, grad_att,
              sums, sum_up, seq_len, direct, parts):
    total, features = low.shape
    four, table = view[0], view[3]
    table_rows = pick_t.shape[0]
    whole = lambda a: pl.BlockSpec(a.shape, lambda i, *_: (0,) * a.ndim, pipeline_mode=pl.Buffered(1))
    weight = lambda g: weight_view(view, g, COLUMNS)
    columns = lambda rows: pl.BlockSpec((rows, COLUMNS), lambda i, *_: (0, i))
    turned = pl.BlockSpec((COLUMNS, key_off.shape[1]), lambda i, *_: (i, 0))
    fixed = lambda s: pl.BlockSpec(s, lambda i, *_: (0,) * len(s))
    shape = jax.ShapeDtypeStruct
    small = (16, features)
    scratch = [pltpu.VMEM((total, features), f32), pltpu.VMEM((table_rows, features), f32)]
    if direct:
        out_specs = [fixed(parts), fixed(parts), fixed((total, features))]
        out_shape = [shape(parts, bf), shape(parts, bf), shape((total, features), bf)]
        scratch.append(pltpu.VMEM(small, f32))
    else:
        out_specs = [pl.BlockSpec((4, features, COLUMNS), lambda i, *_: (0, 0, i)), fixed((table_rows, features)),
                     fixed(small), fixed((total, features))]
        out_shape = [shape((4, features, features), bf), shape((table_rows, features), bf), shape(small, f32),
                     shape((total, features), bf)]
    return pl.pallas_call(
        lambda *refs: unproject_kernel(*refs, seq_len=seq_len, direct=direct),
        grid_spec=pltpu.PrefetchScalarGridSpec(
            num_scalar_prefetch=2,
            grid=(features // COLUMNS,),
            in_specs=[whole(low), columns(total), columns(total), columns(total), turned, turned,
                      weight(0), weight(1), weight(2), table_view(view), whole(pick_t), whole(grad_first),
                      whole(context_t), columns(total), whole(sums), whole(sum_up)],
            out_specs=out_specs,
            scratch_shapes=scratch,
        ),
        out_shape=out_shape,
        compiler_params=pltpu.CompilerParams(vmem_limit_bytes=VMEM_LIMIT),
        cost_estimate=pl.CostEstimate(
            flops=2 * features * features * (7 * total + 4 * table_rows) + 8 * total * features * table_rows,
            bytes_accessed=2 * features * (7 * features + 10 * total), transcendentals=0),
    )(boundary, core, low, dq, dk, dv, key_off, query_off, four, four, four, table, pick_t, grad_first, context_t,
      grad_att, sums, sum_up)


ROWS = 256
CHUNK = 512


def normalize(values):
    centred = values - jnp.mean(values, -1, keepdims=True)
    inverse = lax.rsqrt(jnp.mean(centred * centred, -1, keepdims=True) + NORM_EPS)
    return centred * inverse, inverse


def normalize_back(grad, normed, inverse):
    return inverse * (
        grad
        - jnp.mean(grad, -1, keepdims=True)
        - normed * jnp.mean(grad * normed, -1, keepdims=True)
    )


def ffn_kernel(
    bound_ref, context_ref, tokens_ref, grad_ref, w_o_ref, w_u_ref, w_d_ref, vec_ref, v_up_ref,
    out_ref, hidden_ref, active_ref, grad_ffn_ref, grad_raised_ref, grad_first_ref, grad_att_ref,
    grad_ctx_ref, sums_ref, sum_up_ref, slope_ref, *, seq_len,
):
    step = pl.program_id(0)
    rows = tokens_ref.shape[0]
    wide = w_u_ref.shape[1]
    vec = lambda k: vec_ref[k : k + 1, :]
    v_out, g_first, s_first, v_down, g_second, s_second = [vec(k) for k in range(3, 9)]
    seq = step * rows // seq_len
    pos = step * rows - seq * seq_len + lax.broadcasted_iota(jnp.int32, (rows, 1), 0)
    second = pos >= bound_ref[seq]
    summed = tokens_ref[...].astype(f32) + jnp.where(second, vec(10), vec(9))
    first_normed, first_inverse = normalize(summed + tn(context_ref[...], w_o_ref[...].reshape(tokens_ref.shape[1], -1)) + v_out)
    hidden = first_normed * g_first + s_first
    hidden_low = hidden.astype(bf)
    hidden_ref[...] = hidden_low
    for c in range(0, wide, CHUNK):
        at = slice(c, c + CHUNK)
        raised = nn(hidden_low, w_u_ref[:, at]) + v_up_ref[:, at]
        cumulative = 0.5 + 0.5 * lax.erf(raised * (1.0 / math.sqrt(2.0)))
        active_ref[:, at] = (raised * cumulative).astype(bf)
        density = jnp.exp(-0.5 * raised * raised) * (1.0 / math.sqrt(2.0 * math.pi))
        slope_ref[:, at] = cumulative + raised * density
    second_normed, second_inverse = normalize(hidden + nn(active_ref[...], w_d_ref[...]) + v_down)
    out_ref[...] = (second_normed * g_second + s_second).astype(bf)
    grad = grad_ref[...].astype(f32)
    grad_mixed = normalize_back(grad * g_second, second_normed, second_inverse)
    grad_ffn = grad_mixed.astype(bf)
    grad_ffn_ref[...] = grad_ffn

    @pl.when(step == 0)
    def _():
        sums_ref[...] = jnp.zeros_like(sums_ref)
        sum_up_ref[...] = jnp.zeros_like(sum_up_ref)

    def add_sum(k, values):
        sums_ref[k : k + 1, :] += jnp.sum(values, 0, keepdims=True)

    add_sum(0, grad * second_normed)
    add_sum(1, grad)
    add_sum(2, grad_ffn.astype(f32))
    for c in range(0, wide, CHUNK):
        at = slice(c, c + CHUNK)
        grad_raised = (nt(grad_ffn, w_d_ref[at, :]) * slope_ref[:, at]).astype(bf)
        grad_raised_ref[:, at] = grad_raised
        sum_up_ref[:, at] += jnp.sum(grad_raised.astype(f32), 0, keepdims=True)
    grad_hidden = nt(grad_raised_ref[...], w_u_ref[...]) + grad_mixed
    add_sum(3, grad_hidden * first_normed)
    add_sum(4, grad_hidden)
    grad_first = normalize_back(grad_hidden * g_first, first_normed, first_inverse)
    grad_first_ref[...] = grad_first
    grad_att = grad_first.astype(bf)
    grad_att_ref[...] = grad_att
    add_sum(5, grad_att.astype(f32))
    grad_ctx_ref[...] = nt(w_o_ref[...].reshape(tokens_ref.shape[1], -1), grad_att).astype(bf)


def ffn(boundary, context_t, tokens, out_grad, view, w_u, w_d, vec, v_up, seq_len):
    total, features = tokens.shape
    wide = w_u.shape[1]
    whole = lambda a: pl.BlockSpec(a.shape, lambda i, _: (0, 0), pipeline_mode=pl.Buffered(1))
    narrow = pl.BlockSpec((ROWS, features), lambda i, _: (i, 0))
    broad = pl.BlockSpec((ROWS, wide), lambda i, _: (i, 0))
    turned = pl.BlockSpec((features, ROWS), lambda i, _: (0, i))
    shape = jax.ShapeDtypeStruct
    return pl.pallas_call(
        lambda *refs: ffn_kernel(*refs, seq_len=seq_len),
        grid_spec=pltpu.PrefetchScalarGridSpec(
            num_scalar_prefetch=1,
            grid=(total // ROWS,),
            in_specs=[turned, narrow, narrow, weight_view(view, 3, features), whole(w_u), whole(w_d), whole(vec), whole(v_up)],
            out_specs=[
                narrow, narrow, broad, narrow, broad, narrow, narrow, turned,
                pl.BlockSpec((8, features), lambda i, _: (0, 0)),
                pl.BlockSpec((1, wide), lambda i, _: (0, 0)),
            ],
            scratch_shapes=[pltpu.VMEM((ROWS, wide), f32)],
        ),
        out_shape=[
            shape((total, features), bf), shape((total, features), bf), shape((total, wide), bf),
            shape((total, features), bf), shape((total, wide), bf), shape((total, features), f32),
            shape((total, features), bf), shape((features, total), bf),
            shape((8, features), f32), shape((1, wide), f32),
        ],
        compiler_params=pltpu.CompilerParams(vmem_limit_bytes=VMEM_LIMIT),
        cost_estimate=pl.CostEstimate(
            flops=2 * total * features * (4 * wide + 2 * features),
            bytes_accessed=2 * (2 * features * wide + 2 * total * wide + 8 * total * features),
            transcendentals=2 * total * wide),
    )(boundary, context_t, tokens, out_grad, view[0], w_u, w_d, vec, v_up)


def outer_kernel(left_ref, right_ref, out_ref):
    out_ref[0] = tn(left_ref[...], right_ref[...]).astype(bf)


def outer(left, right, cut_left):
    total, features = left.shape if not cut_left else right.shape
    blocks = (left if cut_left else right).shape[1] // features
    moving = pl.BlockSpec((total, features), lambda i: (0, i))
    fixed = pl.BlockSpec((total, features), lambda i: (0, 0), pipeline_mode=pl.Buffered(1))
    return pl.pallas_call(
        outer_kernel,
        grid=(blocks,),
        in_specs=[moving, fixed] if cut_left else [fixed, moving],
        out_specs=pl.BlockSpec((1, features, features), lambda i: (i, 0, 0)),
        out_shape=jax.ShapeDtypeStruct((blocks, features, features), bf),
        compiler_params=pltpu.CompilerParams(vmem_limit_bytes=VMEM_LIMIT),
        cost_estimate=pl.CostEstimate(
            flops=2 * total * features * features * blocks,
            bytes_accessed=2 * blocks * features * (features + total), transcendentals=0),
    )(left, right)


TILE = 16


def swap_core(a):
    n = lax.axis_size("fsdp")
    return lax.ppermute(a, "fsdp", [(i, i ^ 1) for i in range(n)])


def swap_line(a):
    n = lax.axis_size("fsdp")
    groups = [list(range(c, n, 2)) for c in range(2)]
    return lax.all_to_all(a, "fsdp", 0, 0, tiled=True, axis_index_groups=groups)


def along_line(a, step):
    n = lax.axis_size("fsdp")
    return lax.ppermute(a, "fsdp", [(i, i + 2 * step) for i in range(n) if 0 <= i + 2 * step < n])


def swap_rep(a):
    return lax.all_to_all(a, "rep", 0, 0, tiled=True)


def flip_rep(a, bit):
    return lax.ppermute(a, "rep", [(i, i ^ bit) for i in range(lax.axis_size("rep"))])


def after(a, *others):
    return lax.optimization_barrier((a,) + others)[0]


def spread(a, copies):
    return jnp.broadcast_to(a[None], (copies,) + a.shape)


def gather_rep(a):
    reps = lax.axis_size("rep")
    bits = [1 << k for k in range(reps.bit_length() - 1)]
    width = a.shape[-1] // len(bits)
    me = lax.axis_index("rep")
    shares = []
    for k in range(len(bits)):
        share = a[None, ..., k * width : (k + 1) * width]
        order = bits[k:] + bits[:k]
        for bit in order:
            other = flip_rep(share, bit)
            high = (me // bit) % 2 == 1
            share = jnp.concatenate([jnp.where(high, other, share), jnp.where(high, share, other)])
        at = np.zeros(reps, np.int32)
        for place in range(reps):
            rep = sum(bit for i, bit in enumerate(order) if (place >> i) & 1)
            at[rep] = place
        shares.append(jnp.stack([share[int(p)] for p in at]))
    return jnp.concatenate(shares, axis=-1)


def gather_parts(mine, shard, *others):
    places = lax.axis_size("fsdp") // 2
    place = lax.axis_index("fsdp") // 2
    steps = [k for d in range(1, places) for k in (d, -d)]
    seen = {-k: along_line(mine, k) for k in steps}
    line = jnp.stack([seen[k] for k in range(1 - places, places) if k])
    line = lax.dynamic_slice_in_dim(line, places - 1 - place, places - 1, 0)
    line, *others = lax.optimization_barrier((line, *others))
    every = gather_rep(line)
    at = jnp.arange(places)[:, None, None, None]
    every = every.swapaxes(0, 1)
    before = jnp.pad(every, ((0, 1), (0, 0), (0, 0), (0, 0)))
    behind = jnp.pad(every, ((1, 0), (0, 0), (0, 0), (0, 0)))
    every = jnp.where(at == place, shard[None], jnp.where(at < place, before, behind))
    other = swap_core(every)
    first = lax.axis_index("fsdp") % 2 == 0
    return jnp.stack([jnp.where(first, every, other), jnp.where(first, other, every)], axis=1), others


def summed_over(a):
    return jnp.sum(a.astype(f32), 0).astype(bf)


def pad_tail(a, rows, columns):
    return jnp.pad(a, [(0, 0)] * (a.ndim - 2) + [(0, rows - a.shape[-2]), (0, columns - a.shape[-1])])


def per_device(
    tokens, lengths, boundary,
    w_query, b_query, w_key, b_key, w_value, b_value, w_out, b_out,
    first_gain, first_shift, w_up, b_up, w_down, b_down,
    second_gain, second_shift, rel_table, type_table, out_grad,
):
    micros, seqs, seq_len, features = tokens.shape
    rows = micros * seqs * seq_len
    heads = features // HEAD_DIM
    fs, reps = lax.axis_size("fsdp"), lax.axis_size("rep")
    places = fs // 2
    cut = w_query.shape[0]
    unit = 4 * cut // reps
    table_cut = rel_table.shape[0] // reps
    up_parts = w_up.shape[1] // features
    vectors = jnp.stack([b_query, b_key, b_value, b_out, first_gain, first_shift, b_down, second_gain,
                         second_shift, type_table[0], type_table[1]] + [b_up[k * cut : (k + 1) * cut] for k in range(up_parts)])
    vector_count = vectors.shape[0]
    vector_rows = -(-vector_count // TILE) * TILE
    vectors = pad_tail(vectors, vector_rows, features)
    shard = jnp.concatenate([
        jnp.stack([w_query, w_key, w_value, w_out]).reshape(reps, unit, features),
        rel_table.reshape(reps, table_cut, features),
        spread(vectors, reps)], axis=1)
    mine = lax.dynamic_index_in_dim(shard, lax.axis_index("rep"), 0, keepdims=False)
    first, (w_up, w_down) = gather_parts(mine, shard, w_up, w_down)
    w_u = lax.all_gather(w_up, "fsdp", axis=0, tiled=True)
    w_d = lax.all_gather(w_down, "fsdp", axis=0, tiled=True)
    direct = unit if unit == cut and cut % TILE == 0 and table_cut % TILE == 0 else 0
    part = unit + table_cut + vector_rows
    if direct:
        view = (first, (places, 2), cut, first, (places, 2, reps, table_cut, features), (0, 0, 0, unit // table_cut, 0))
    else:
        four = first[:, :, :, :unit].reshape(fs, 4, reps // 4, unit, features).transpose(1, 0, 2, 3, 4)
        rel = first[:, :, :, unit : unit + table_cut].reshape(1, 1, 1, -1, features)
        view = (four.reshape(1, 1, 4, features, features), (1, 1), features, rel, rel.shape, (0,) * 5)
    wide = first[:, :, 0, unit + table_cut : unit + table_cut + vector_count, :cut].reshape(fs, vector_count, cut)
    wide = wide.transpose(1, 0, 2).astype(f32)
    v_up = wide[vector_count - up_parts :].transpose(1, 0, 2).reshape(1, -1)
    wide = wide.reshape(vector_count, features)

    offsets = np.clip(np.arange(2 * seq_len) - (seq_len - 1), 1 - seq_len, seq_len - 1)
    pick = pick_rows(offsets)
    pick_back = pick_rows(-offsets)
    flat_bound, flat_lengths = boundary.reshape(-1), lengths.reshape(-1)
    flat_tokens, flat_grad = tokens.reshape(rows, features), out_grad.reshape(rows, features)
    queries, keys, values, key_rows, query_rows, key_back_t, query_t, summed_low = project(
        flat_bound, flat_tokens, view, jnp.asarray(pick, bf), jnp.asarray(pick.T, bf), jnp.asarray(pick_back.T, bf),
        wide, wide[9:11], seq_len)
    context_t, probs, inverse_total = attn_fwd(
        queries, keys, values, key_back_t, query_t, flat_lengths, heads)
    (layer_out, hidden_low, active, grad_ffn, grad_raised, grad_first, grad_attended, grad_context_t,
     sums, sum_up) = ffn(flat_bound, context_t, flat_tokens, flat_grad, view, w_u, w_d, wide, v_up, seq_len)
    d_down = outer(active, grad_ffn, True).reshape(-1, features)
    s_down = lax.psum_scatter(d_down, "fsdp", scatter_dimension=0, tiled=True)
    s_up = lax.psum_scatter(outer(hidden_low, grad_raised, False), "fsdp", scatter_dimension=1, tiled=True)
    d_query, d_key, d_value, key_off, query_off = attn_bwd(
        queries, keys, values, grad_context_t, probs, inverse_total, key_rows, query_rows)
    core = lax.axis_index("fsdp") % 2
    *made, tokens_grad = unproject(
        flat_bound, core.reshape(1), summed_low, d_query, d_key, d_value, key_off, query_off, view,
        jnp.asarray(pick.T, bf), grad_first, context_t, grad_attended, sums, sum_up, seq_len, direct,
        (reps, places, part, features))
    if direct:
        keep, give = made
    else:
        four, d_rel, small = made
        four = four.reshape(4, places, 2, reps // 4, unit, features).transpose(0, 3, 1, 2, 4, 5)
        small = jnp.broadcast_to(small.astype(bf), (reps, places, 2) + small.shape)
        last = jnp.concatenate([
            four.reshape(reps, places, 2, unit, features),
            d_rel.reshape(places, 2, reps, table_cut, features).transpose(2, 0, 1, 3, 4), small], axis=3)
        keep = lax.dynamic_index_in_dim(last, core, 2, keepdims=False)
        give = lax.dynamic_index_in_dim(last, 1 - core, 2, keepdims=False)
    last = (keep.astype(f32) + swap_core(give).astype(f32)).astype(bf)
    early = jnp.concatenate([s_down, s_up.reshape(-1, features)])
    early = lax.psum_scatter(early, "rep", scatter_dimension=0, tiled=True)
    last = summed_over(swap_rep(last))
    early = after(early, last)
    early = lax.all_gather(early, "rep", axis=0, tiled=True)
    last = summed_over(swap_line(last))
    small = last[unit + table_cut : unit + table_cut + vector_count].astype(f32)
    small = lax.dynamic_slice_in_dim(small[: vector_count - up_parts], lax.axis_index("fsdp") * cut, cut, 1)
    d_b_up = last[unit + table_cut + vector_count - up_parts : unit + table_cut + vector_count].astype(f32)
    d_b_up = lax.dynamic_slice_in_dim(d_b_up.reshape(-1), lax.axis_index("fsdp") * up_parts * cut, up_parts * cut, 0)
    both = swap_rep(spread(last[: unit + table_cut], reps)).astype(f32)
    four = both[:, :unit].reshape(4, cut, features)
    s_q, s_k, s_v, s_o = four[0], four[1], four[2], four[3]
    s_rel = both[:, unit:].reshape(-1, features)
    (d_b_query, d_b_key, d_b_value, d_b_out, d_first_gain, d_first_shift, d_b_down,
     d_second_gain, d_second_shift, d_type_zero, d_type_one) = [
        small[k] for k in range(vector_count - up_parts)]
    s_down = early[: w_down.shape[0]].astype(f32)
    s_up = early[w_down.shape[0] :].reshape(up_parts, cut, features).transpose(1, 0, 2)
    s_up = s_up.reshape(cut, -1).astype(f32)
    return (
        layer_out.reshape(tokens.shape), tokens_grad.reshape(tokens.shape),
        s_q, d_b_query, s_k, d_b_key, s_v, d_b_value, s_o, d_b_out,
        d_first_gain, d_first_shift, s_up, d_b_up, s_down, d_b_down,
        d_second_gain, d_second_shift, s_rel, jnp.stack([d_type_zero, d_type_one]),
    )


def solution(mesh):
    seq = P(None, ("rep", "fsdp"), None, None)
    flat = P(None, ("rep", "fsdp"))
    mat, vec = P("fsdp", None), P("fsdp")
    weights = (mat, vec, mat, vec, mat, vec, mat, vec, vec, vec, mat, vec, mat, vec, vec, vec, mat,
               P(None, "fsdp"))
    return jax.shard_map(
        per_device,
        mesh=mesh,
        in_specs=(seq, flat, flat) + weights + (seq,),
        out_specs=(seq, seq) + weights,
        check_vma=False,
    )
```

```python
import math

import jax
import jax.numpy as jnp
import numpy as np
from jax import lax
from jax.experimental import pallas as pl
from jax.experimental.pallas import tpu as pltpu
from jax.sharding import PartitionSpec as P

BUCKETS = 256
MAX_POS = 512
NORM_EPS = 1e-07
VMEM_LIMIT = 62 * 1024 * 1024

HEAD_DIM=64
MASKED=-1e30
f32=jnp.float32; bf=jnp.bfloat16
BLK=128
LOG2E=math.log2(math.e)

def nn(a,b): return lax.dot_general(a,b,(((1,),(0,)),((),())),preferred_element_type=f32)
def nt(a,b): return lax.dot_general(a,b,(((1,),(1,)),((),())),preferred_element_type=f32)

def eye(rows, flip=False):
    r=lax.broadcasted_iota(jnp.int32,(rows,rows),0)
    c=lax.broadcasted_iota(jnp.int32,(rows,rows),1)
    return jnp.where((r+c==rows-1) if flip else (r==c),1.0,0.0).astype(bf)

def attn_fwd_kernel(len_ref,q_ref,k_ref,v_ref,pkrT_ref,pqT_ref,ctxT_ref,p_ref,linv_ref,c_scr,s_scr):
    S=q_ref.shape[0]
    nb=S//BLK
    W=S+BLK
    m=pl.program_id(1)
    length=len_ref[m]
    scale=LOG2E/math.sqrt(3*HEAD_DIM)
    q=q_ref[...]; k=k_ref[...]
    pqT=pqT_ref[...]
    vT=v_ref[...].T; qT=q.T
    row_h=lax.broadcasted_iota(jnp.int32,(2*HEAD_DIM,S),0)
    lane_s=lax.broadcasted_iota(jnp.int32,(S,2*HEAD_DIM),1)
    row_s=lax.broadcasted_iota(jnp.int32,(S,2*HEAD_DIM),0)
    row_t=lax.broadcasted_iota(jnp.int32,(2*HEAD_DIM,2*S),0)
    bias=jnp.where(row_s<length,0.0,MASKED).astype(bf)
    zero=jnp.zeros((),bf)
    pos=lax.broadcasted_iota(jnp.int32,(1,S),1)
    for h in range(2):
        mine=(lane_s<HEAD_DIM) if h==0 else (lane_s>=HEAD_DIM)
        spare=HEAD_DIM if h==0 else 0
        qh=jnp.where(mine,q,zero)
        kb=jnp.where(mine,k,jnp.where(lane_s==spare,bias,zero))
        pqh=jnp.where(row_t==spare,jnp.ones((),bf),pqT)
        qTh=jnp.where((row_h<HEAD_DIM) if h==0 else (row_h>=HEAD_DIM),qT,zero)
        for b in range(nb):
            st=(nb-1-b)*BLK
            c=nn(qh[b*BLK:(b+1)*BLK],pkrT_ref[:,st:st+W]).astype(bf)
            c_scr[h,b*BLK:(b+1)*BLK,:]=pltpu.roll(c,S+1,1,stride=1,stride_axis=0)[:,:S]
        top=None
        for b in range(nb):
            st=(nb-1-b)*BLK
            js=slice(b*BLK,(b+1)*BLK)
            d=nn(kb[js],pqh[:,st:st+W]).astype(bf)
            d=pltpu.roll(d,S+1,1,stride=1,stride_axis=0)[:,:S]
            s=nn(k[js],qTh)+(c_scr[h,:,js].T.astype(f32)+d.astype(f32))
            s_scr[h,js,:]=s
            t=jnp.max(s,axis=0,keepdims=True)
            top=t if top is None else jnp.maximum(top,t)
        top=top*scale
        tot=None
        for b in range(nb):
            js=slice(b*BLK,(b+1)*BLK)
            p=jnp.exp2(s_scr[h,js,:]*scale-top).astype(bf)
            t=jnp.sum(p.astype(f32),axis=0,keepdims=True)
            tot=t if tot is None else tot+t
            p_ref[0,h,js,:]=p
        linv=jnp.where(pos<length,1.0/tot,0.0)
        linv_ref[0,0,h:h+1,:]=linv
        ctx=nn(vT[h*HEAD_DIM:(h+1)*HEAD_DIM,:],p_ref[0,h])*linv
        ctxT_ref[h*HEAD_DIM:(h+1)*HEAD_DIM,:]=ctx.astype(bf)

def attn_fwd(q,k,v,pkr,pq,lengths,heads):
    M=lengths.shape[0]; D=heads*HEAD_DIM
    S=pq.shape[1]//2
    NP=heads//2; L=2*HEAD_DIM
    grid=(NP,M)
    return pl.pallas_call(
        attn_fwd_kernel,
        grid_spec=pltpu.PrefetchScalarGridSpec(
            num_scalar_prefetch=1,grid=grid,
            in_specs=[
                pl.BlockSpec((S,L),lambda p,m,_:(m,p)),
                pl.BlockSpec((S,L),lambda p,m,_:(m,p)),
                pl.BlockSpec((S,L),lambda p,m,_:(m,p)),
                pl.BlockSpec((L,2*S),lambda p,m,_:(p,0)),
                pl.BlockSpec((L,2*S),lambda p,m,_:(p,0)),
            ],
            out_specs=[
                pl.BlockSpec((L,S),lambda p,m,_:(p,m)),
                pl.BlockSpec((1,2,S,S),lambda p,m,_:(m,p,0,0)),
                pl.BlockSpec((1,1,2,S),lambda p,m,_:(m,p,0,0)),
            ],
            scratch_shapes=[pltpu.VMEM((2,S,S),bf),pltpu.VMEM((2,S,S),f32)],
        ),
        out_shape=[jax.ShapeDtypeStruct((D,M*S),bf),jax.ShapeDtypeStruct((M,heads,S,S),bf),jax.ShapeDtypeStruct((M,NP,2,S),f32)],
        compiler_params=pltpu.CompilerParams(vmem_limit_bytes=VMEM_LIMIT),
        cost_estimate=pl.CostEstimate(flops=int(2*M*heads*S*S*64*12),bytes_accessed=int(M*heads*S*S*2),transcendentals=M*heads*S*S),
    )(lengths,q,k,v,pkr,pq)

def attn_bwd_kernel(q_ref,k_ref,v_ref,dcT_ref,p_ref,linv_ref,pk_ref,pq_ref,dq_ref,dk_ref,dv_ref,ko_out,qo_out,ds_scr,p_scr,t_scr,ko_ref,qo_ref):
    S=q_ref.shape[0]
    nb=S//BLK
    W=S+BLK
    m=pl.program_id(1)
    scale=1.0/math.sqrt(3*HEAD_DIM)
    zero=jnp.zeros((),bf)
    flip=eye(BLK,True)
    q=q_ref[...]
    def reverse(x):
        return jnp.concatenate([nn(flip,x[(nb-1-b)*BLK:(nb-b)*BLK]).astype(bf) for b in range(nb)],axis=0)
    kr=reverse(k_ref[...]); vr=reverse(v_ref[...])
    qT=q.T; krT=kr.T
    lane_s=lax.broadcasted_iota(jnp.int32,(S,2*HEAD_DIM),1)
    lane_t=lax.broadcasted_iota(jnp.int32,(2*S,2*HEAD_DIM),1)
    pad=jnp.zeros((BLK,BLK),bf)
    @pl.when(m==0)
    def _():
        ko_ref[...]=jnp.zeros_like(ko_ref)
        qo_ref[...]=jnp.zeros_like(qo_ref)
    dq=[None]*nb; dk=[None]*nb; dv=None
    zrow=jnp.zeros((HEAD_DIM,S),bf)
    for h in range(2):
        hs=slice(h*HEAD_DIM,(h+1)*HEAD_DIM)
        mine=(lane_s<HEAD_DIM) if h==0 else (lane_s>=HEAD_DIM)
        mine_t=(lane_t<HEAD_DIM) if h==0 else (lane_t>=HEAD_DIM)
        qh=jnp.where(mine,q,zero); krh=jnp.where(mine,kr,zero)
        pkh=jnp.where(mine_t,pk_ref[...],zero); pqh=jnp.where(mine_t,pq_ref[...],zero)
        linv=linv_ref[0,0,h:h+1,:]
        dc=dcT_ref[hs,:].astype(f32)*linv
        dcl=dc.astype(bf); dcs=(dc*scale).astype(bf)
        def wide(x): return jnp.concatenate([x,zrow] if h==0 else [zrow,x],axis=0)
        t=nt(p_ref[0,h],wide(dcl))
        dv=t if dv is None else dv+t
        dcw=wide(dcs)
        delta=None
        dp=nn(vr,dcw)
        for b in range(nb):
            js=slice(b*BLK,(b+1)*BLK)
            p=nn(flip,p_ref[0,h,(nb-1-b)*BLK:(nb-b)*BLK,:])
            t=p*dp[js]
            p_scr[h,js,:]=p
            t_scr[h,js,:]=t
            t=jnp.sum(t,axis=0,keepdims=True)
            delta=t if delta is None else delta+t
        delta=delta*linv
        for b in range(nb):
            js=slice(b*BLK,(b+1)*BLK)
            ds=(t_scr[h,js,:]-p_scr[h,js,:]*delta).astype(bf)
            ds_scr[h,js,:]=ds
            far=pltpu.roll(jnp.concatenate([ds,pad],axis=1),0,1,stride=1,stride_axis=0)
            st=b*BLK
            t=nn(ds,qh)+nn(far,pqh[st:st+W])
            dk[b]=t if dk[b] is None else dk[b]+t
            qo_ref[hs,st:st+W]+=nn(krT[hs,js],far)
        for b in range(nb):
            js=slice(b*BLK,(b+1)*BLK)
            ds=ds_scr[h,:,js].T
            near=pltpu.roll(jnp.concatenate([ds,pad],axis=1),0,1,stride=1,stride_axis=0)
            st=b*BLK
            t=nn(ds,krh)+nn(near,pkh[st:st+W])
            dq[b]=t if dq[b] is None else dq[b]+t
            ko_ref[hs,st:st+W]+=nn(qT[hs,js],near)
    @pl.when(m==pl.num_programs(1)-1)
    def _():
        ko_out[...]=ko_ref[...].astype(bf)
        qo_out[...]=qo_ref[...].astype(bf)
    dv_ref[...]=dv.astype(bf)
    for b in range(nb):
        dq_ref[b*BLK:(b+1)*BLK,:]=dq[b].astype(bf)
        dk_ref[(nb-1-b)*BLK:(nb-b)*BLK,:]=nn(flip,dk[b].astype(bf)).astype(bf)

def attn_bwd(q,k,v,dcT,p,linv,pk,pq):
    M,heads,S,_=p.shape; D=heads*HEAD_DIM
    NP=heads//2; L=2*HEAD_DIM
    tok=lambda off: pl.BlockSpec((S,L),lambda p,m:(m,off+p))
    colT=pl.BlockSpec((L,S),lambda p,m:(p,m))
    tab=pl.BlockSpec((2*S,L),lambda p,m:(0,p))
    return pl.pallas_call(
        attn_bwd_kernel,
        grid=(NP,M),
        in_specs=[tok(0),tok(0),tok(0),colT,
            pl.BlockSpec((1,2,S,S),lambda p,m:(m,p,0,0)),
            pl.BlockSpec((1,1,2,S),lambda p,m:(m,p,0,0)),
            tab,tab],
        out_specs=[tok(0),tok(0),tok(0),pl.BlockSpec((L,2*S),lambda p,m:(p,0)),pl.BlockSpec((L,2*S),lambda p,m:(p,0))],
        out_shape=[jax.ShapeDtypeStruct((M*S,D),bf)]*3+[jax.ShapeDtypeStruct((D,2*S),bf)]*2,
        scratch_shapes=[pltpu.VMEM((2,S,S),bf),pltpu.VMEM((2,S,S),f32),pltpu.VMEM((2,S,S),f32),pltpu.VMEM((L,2*S),f32),pltpu.VMEM((L,2*S),f32)],
        compiler_params=pltpu.CompilerParams(vmem_limit_bytes=VMEM_LIMIT),
        cost_estimate=pl.CostEstimate(flops=int(2*M*heads*S*S*64*24),bytes_accessed=int(M*heads*S*S*2),transcendentals=0),
    )(q,k,v,dcT,p,linv,pk,pq)


def bucket_index(offset_of):
    middle = BUCKETS // 2
    sign_of = np.sign(offset_of)
    magnitude = np.where(
        (offset_of < middle) & (offset_of > -middle), middle - 1, np.abs(offset_of)
    )
    log_pos = (
        np.ceil(np.log(magnitude / middle) / np.log((MAX_POS - 1) / middle) * (middle - 1)) + middle
    )
    bucket = np.where(magnitude <= middle, offset_of, log_pos * sign_of)
    return np.clip(bucket + BUCKETS, 0, 2 * BUCKETS - 1)


def pick_rows(offsets):
    return (bucket_index(offsets)[:, None] == np.arange(2 * BUCKETS)[None, :]).astype(np.float32)


def tn(a, b):
    return lax.dot_general(a, b, (((0,), (0,)), ((), ())), preferred_element_type=f32)

COLUMNS = 256


def second_rows(bound_ref, rows, seq_len):
    at = lax.broadcasted_iota(jnp.int32, (rows, 1), 0)
    second = at < 0
    for m in range(rows // seq_len):
        second = second | ((at >= m * seq_len + bound_ref[m]) & (at < (m + 1) * seq_len))
    return second


def project_kernel(
    bound_ref, core_ref, tokens_ref, w_q_ref, w_q2_ref, w_k_ref, w_k2_ref, w_v_ref, w_v2_ref, rel_ref, rel2_ref,
    pick_ref, pick_t_ref, pick_back_t_ref, vec_ref,
    type_ref, q_ref, k_ref, v_ref, key_ref, query_ref, key_back_ref, query_t_ref, low_ref, *, seq_len,
):
    rows = tokens_ref.shape[0]

    @pl.when(pl.program_id(0) == 0)
    def _():
        second = second_rows(bound_ref, rows, seq_len)
        low_ref[...] = (
            tokens_ref[...].astype(f32) + jnp.where(second, type_ref[1:2, :], type_ref[0:1, :])
        ).astype(bf)

    low = low_ref[...]
    first = core_ref[0] == 0
    rel = in_order(rel_ref, rel2_ref, first, pick_ref.shape[1])
    features = tokens_ref.shape[1]
    w_q = in_order(w_q_ref, w_q2_ref, first, features)
    w_k = in_order(w_k_ref, w_k2_ref, first, features)
    w_v = in_order(w_v_ref, w_v2_ref, first, features)
    b_q, b_k = vec_ref[0:1, :], vec_ref[1:2, :]
    q_ref[...] = (nn(low, w_q) + b_q).astype(bf)
    k_ref[...] = (nn(low, w_k) + b_k).astype(bf)
    v_ref[...] = (nn(low, w_v) + vec_ref[2:3, :]).astype(bf)
    pos_query = (nn(rel, w_q) + b_q).astype(bf)
    pos_key = (nn(rel, w_k) + b_k).astype(bf)
    query_ref[...] = nn(pick_ref[...], pos_query).astype(bf)
    key_ref[...] = nn(pick_ref[...], pos_key).astype(bf)
    key_back_ref[...] = tn(pos_key, pick_back_t_ref[...]).astype(bf)
    query_t_ref[...] = tn(pos_query, pick_t_ref[...]).astype(bf)


def weight_view(view, g, columns):
    spec = pl.BlockSpec((view[0].shape[0], 1, view[2], columns), lambda i, *_: (0, g, 0, i if columns == COLUMNS else 0),
                        pipeline_mode=None if columns == COLUMNS else pl.Buffered(1))
    return [spec, spec]


def table_view(view):
    spec = pl.BlockSpec(view[5], lambda i, *_: view[6], pipeline_mode=pl.Buffered(1))
    return [spec, spec]


def in_order(own_ref, other_ref, first, rows):
    own = own_ref[...]
    columns = own.shape[-1]
    if own.size == rows * columns:
        return own.reshape(rows, columns)
    other = other_ref[...]
    both = jnp.stack([jnp.where(first, own, other), jnp.where(first, other, own)], axis=1)
    return both.reshape(rows, columns)


def project(boundary, core, tokens, view, pick, pick_t, pick_back_t, vec, types, seq_len):
    total, features = tokens.shape
    table_rows = pick.shape[1]
    whole = lambda a: pl.BlockSpec(a.shape, lambda i, *_: (0,) * a.ndim, pipeline_mode=pl.Buffered(1))
    weight = lambda g: weight_view(view, g, COLUMNS)
    columns = lambda rows: pl.BlockSpec((rows, COLUMNS), lambda i, *_: (0, i))
    shape = jax.ShapeDtypeStruct
    offsets = pick.shape[0]
    return pl.pallas_call(
        lambda *refs: project_kernel(*refs, seq_len=seq_len),
        grid_spec=pltpu.PrefetchScalarGridSpec(
            num_scalar_prefetch=2,
            grid=(features // COLUMNS,),
            in_specs=[whole(tokens), *weight(0), *weight(1), *weight(2), *table_view(view), whole(pick),
                      whole(pick_t), whole(pick_back_t), columns(vec.shape[0]), whole(types)],
            out_specs=[columns(total)] * 3 + [columns(offsets)] * 2
            + [pl.BlockSpec((COLUMNS, offsets), lambda i, *_: (i, 0))] * 2
            + [pl.BlockSpec((total, features), lambda i, *_: (0, 0))],
        ),
        out_shape=[shape((total, features), bf)] * 3 + [shape((offsets, features), bf)] * 2
        + [shape((features, offsets), bf)] * 2
        + [shape((total, features), bf)],
        compiler_params=pltpu.CompilerParams(vmem_limit_bytes=VMEM_LIMIT),
        cost_estimate=pl.CostEstimate(
            flops=2 * features * features * (3 * total + 2 * table_rows) + 6 * offsets * features * table_rows,
            bytes_accessed=2 * features * (3 * features + 5 * total + 3 * offsets), transcendentals=0),
    )(boundary, core, tokens, *(view[:2] * 3), *view[3:5], pick, pick_t, pick_back_t, vec, types)


def unproject_kernel(
    bound_ref, core_ref, low_ref, dq_ref, dk_ref, dv_ref, key_off_ref, query_off_ref, w_q_ref, w_q2_ref,
    w_k_ref, w_k2_ref, w_v_ref, w_v2_ref, rel_ref, rel2_ref, pick_t_ref, context_ref, grad_att_ref, sums_ref, sum_up_ref,
    *refs, seq_len, direct,
):
    if direct:
        keep_ref, give_ref, rel_sum_ref, small_ref = refs
    else:
        dw_ref, drel_ref, small_ref, rel_sum_ref = refs
    step = pl.program_id(0)
    rows, features = low_ref.shape
    first = core_ref[0] == 0

    @pl.when(step == 0)
    def _():
        rel_sum_ref[...] = jnp.zeros_like(rel_sum_ref)
        small_ref[...] = jnp.zeros_like(small_ref)
        small_ref[9:11, :] = sums_ref[6:8, :]

    low, rel = low_ref[...], in_order(rel_ref, rel2_ref, first, pick_t_ref.shape[0])
    w_q = in_order(w_q_ref, w_q2_ref, first, features)
    w_k = in_order(w_k_ref, w_k2_ref, first, features)
    w_v = in_order(w_v_ref, w_v2_ref, first, features)
    dq, dk, dv = dq_ref[...], dk_ref[...], dv_ref[...]
    columns = pl.ds(pl.multiple_of(step * COLUMNS, COLUMNS), COLUMNS)

    def put(at, rows_at, values):
        if direct:
            _, places, part, _ = keep_ref.shape
            values = values.astype(bf).reshape(places, 2, -1, values.shape[-1])
            keep_ref[at, :, rows_at, columns] = jnp.where(first, values[:, 0], values[:, 1])
            give_ref[at, :, rows_at, columns] = jnp.where(first, values[:, 1], values[:, 0])
        else:
            dw_ref[at] = values.astype(bf)

    unit = direct
    pos_query = nt(pick_t_ref[...], query_off_ref[...])
    pos_key = nt(pick_t_ref[...], key_off_ref[...])
    low_query, low_key = pos_query.astype(bf), pos_key.astype(bf)
    put(0, slice(0, unit), tn(low, dq) + tn(rel, low_query))
    put(1, slice(0, unit), tn(low, dk) + tn(rel, low_key))
    put(2, slice(0, unit), tn(low, dv))
    put(3, slice(0, unit), nn(context_ref[...], grad_att_ref[...]))
    total = lambda a: jnp.sum(a.astype(f32), 0, keepdims=True)
    small_ref[0:1, columns] = total(dq) + total(pos_query)
    small_ref[1:2, columns] = total(dk) + total(pos_key)
    small_ref[2:3, columns] = total(dv)
    second = second_rows(bound_ref, rows, seq_len)
    for values, weight in ((dq, w_q), (dk, w_k), (dv, w_v)):
        wide = values.astype(f32)
        parts = jnp.concatenate([total(jnp.where(second, 0.0, wide)), total(jnp.where(second, wide, 0.0))])
        high = parts.astype(bf)
        low_part = (parts - high.astype(f32)).astype(bf)
        stacked = jnp.concatenate([high, low_part, jnp.zeros((12, parts.shape[1]), bf)])
        product = nt(stacked, weight)
        small_ref[9:11, :] += product[0:2] + product[2:4]
    rel_sum_ref[...] += nt(low_key, w_k) + nt(low_query, w_q)

    @pl.when(step == pl.num_programs(0) - 1)
    def _():
        for at, k in ((3, 5), (4, 3), (5, 4), (6, 2), (7, 0), (8, 1)):
            small_ref[at : at + 1, :] = sums_ref[k : k + 1, :]
        for k in range(sum_up_ref.shape[1] // features):
            small_ref[11 + k : 12 + k, :] = sum_up_ref[:, k * features : (k + 1) * features]
        if direct:
            reps, places, part, _ = keep_ref.shape
            table = rel_sum_ref[...].astype(bf).reshape(places, 2, reps, -1, features)
            small = small_ref[...].astype(bf)
            end = unit + table.shape[3]
            for r in range(reps):
                keep_ref[r, :, unit:end, :] = jnp.where(first, table[:, 0, r], table[:, 1, r])
                give_ref[r, :, unit:end, :] = jnp.where(first, table[:, 1, r], table[:, 0, r])
                for z in range(places):
                    keep_ref[r, z, end:part, :] = small
                    give_ref[r, z, end:part, :] = small
        else:
            drel_ref[...] = rel_sum_ref[...].astype(bf)


def unproject(boundary, core, low, dq, dk, dv, key_off, query_off, view, pick_t, context_t, grad_att,
              sums, sum_up, seq_len, direct, parts):
    total, features = low.shape
    table_rows = pick_t.shape[0]
    whole = lambda a: pl.BlockSpec(a.shape, lambda i, *_: (0,) * a.ndim, pipeline_mode=pl.Buffered(1))
    weight = lambda g: weight_view(view, g, COLUMNS)
    columns = lambda rows: pl.BlockSpec((rows, COLUMNS), lambda i, *_: (0, i))
    turned = pl.BlockSpec((COLUMNS, key_off.shape[1]), lambda i, *_: (i, 0))
    fixed = lambda s: pl.BlockSpec(s, lambda i, *_: (0,) * len(s))
    shape = jax.ShapeDtypeStruct
    small = (16, features)
    scratch = [pltpu.VMEM((table_rows, features), f32)]
    if direct:
        out_specs = [fixed(parts), fixed(parts)]
        out_shape = [shape(parts, bf), shape(parts, bf)]
        scratch.append(pltpu.VMEM(small, f32))
    else:
        out_specs = [pl.BlockSpec((4, features, COLUMNS), lambda i, *_: (0, 0, i)), fixed((table_rows, features)),
                     fixed(small)]
        out_shape = [shape((4, features, features), bf), shape((table_rows, features), bf), shape(small, f32)]
    return pl.pallas_call(
        lambda *refs: unproject_kernel(*refs, seq_len=seq_len, direct=direct),
        grid_spec=pltpu.PrefetchScalarGridSpec(
            num_scalar_prefetch=2,
            grid=(features // COLUMNS,),
            in_specs=[whole(low), columns(total), columns(total), columns(total), turned, turned,
                      *weight(0), *weight(1), *weight(2), *table_view(view), whole(pick_t),
                      whole(context_t), columns(total), whole(sums), whole(sum_up)],
            out_specs=out_specs,
            scratch_shapes=scratch,
        ),
        out_shape=out_shape,
        compiler_params=pltpu.CompilerParams(vmem_limit_bytes=VMEM_LIMIT),
        cost_estimate=pl.CostEstimate(
            flops=2 * features * features * (4 * total + 4 * table_rows) + 8 * total * features * table_rows,
            bytes_accessed=2 * features * (7 * features + 10 * total), transcendentals=0),
    )(boundary, core, low, dq, dk, dv, key_off, query_off, *(view[:2] * 3), *view[3:5], pick_t,
      context_t, grad_att, sums, sum_up)


def token_kernel(core_ref, dq_ref, dk_ref, dv_ref, w_q_ref, w_q2_ref, w_k_ref, w_k2_ref, w_v_ref, w_v2_ref,
                 grad_first_ref, grad_ref):
    first, features = core_ref[0] == 0, dq_ref.shape[1]
    grad_ref[...] = (
        nt(dq_ref[...], in_order(w_q_ref, w_q2_ref, first, features))
        + nt(dk_ref[...], in_order(w_k_ref, w_k2_ref, first, features))
        + nt(dv_ref[...], in_order(w_v_ref, w_v2_ref, first, features)) + grad_first_ref[...]).astype(bf)


def token_grads(core, dq, dk, dv, view, grad_first):
    total, features = dq.shape
    rows = pl.BlockSpec((total // 2, features), lambda i, *_: (i, 0))
    weights = [spec for g in range(3) for spec in weight_view(view, g, features)]
    return pl.pallas_call(
        token_kernel,
        grid_spec=pltpu.PrefetchScalarGridSpec(
            num_scalar_prefetch=1, grid=(2,), in_specs=[rows, rows, rows, *weights, rows], out_specs=rows),
        out_shape=jax.ShapeDtypeStruct((total, features), bf),
        compiler_params=pltpu.CompilerParams(vmem_limit_bytes=VMEM_LIMIT),
        cost_estimate=pl.CostEstimate(
            flops=6 * total * features * features, bytes_accessed=2 * features * (6 * total + 3 * features),
            transcendentals=0),
    )(core, dq, dk, dv, *(view[:2] * 3), grad_first)


ROWS = 256
CHUNK = 512


def normalize(values):
    centred = values - jnp.mean(values, -1, keepdims=True)
    inverse = lax.rsqrt(jnp.mean(centred * centred, -1, keepdims=True) + NORM_EPS)
    return centred * inverse, inverse


def normalize_back(grad, normed, inverse):
    return inverse * (
        grad
        - jnp.mean(grad, -1, keepdims=True)
        - normed * jnp.mean(grad * normed, -1, keepdims=True)
    )


def ffn_kernel(
    bound_ref, core_ref, context_ref, tokens_ref, grad_ref, w_o_ref, w_o2_ref, w_u_ref, w_d_ref, vec_ref, v_up_ref,
    out_ref, hidden_ref, active_ref, grad_ffn_ref, grad_raised_ref, grad_first_ref, grad_att_ref,
    grad_ctx_ref, sums_ref, sum_up_ref, slope_ref, *, seq_len,
):
    step = pl.program_id(0)
    rows = tokens_ref.shape[0]
    wide = w_u_ref.shape[1]
    vec = lambda k: vec_ref[k : k + 1, :]
    w_o = in_order(w_o_ref, w_o2_ref, core_ref[0] == 0, tokens_ref.shape[1])
    v_out, g_first, s_first, v_down, g_second, s_second = [vec(k) for k in range(3, 9)]
    seq = step * rows // seq_len
    pos = step * rows - seq * seq_len + lax.broadcasted_iota(jnp.int32, (rows, 1), 0)
    second = pos >= bound_ref[seq]
    summed = tokens_ref[...].astype(f32) + jnp.where(second, vec(10), vec(9))
    first_normed, first_inverse = normalize(summed + tn(context_ref[...], w_o) + v_out)
    hidden = first_normed * g_first + s_first
    hidden_low = hidden.astype(bf)
    hidden_ref[...] = hidden_low
    for c in range(0, wide, CHUNK):
        at = slice(c, c + CHUNK)
        raised = nn(hidden_low, w_u_ref[:, at]) + v_up_ref[:, at]
        cumulative = 0.5 + 0.5 * lax.erf(raised * (1.0 / math.sqrt(2.0)))
        active_ref[:, at] = (raised * cumulative).astype(bf)
        density = jnp.exp(-0.5 * raised * raised) * (1.0 / math.sqrt(2.0 * math.pi))
        slope_ref[:, at] = cumulative + raised * density
    second_normed, second_inverse = normalize(hidden + nn(active_ref[...], w_d_ref[...]) + v_down)
    out_ref[...] = (second_normed * g_second + s_second).astype(bf)
    grad = grad_ref[...].astype(f32)
    grad_mixed = normalize_back(grad * g_second, second_normed, second_inverse)
    grad_ffn = grad_mixed.astype(bf)
    grad_ffn_ref[...] = grad_ffn

    @pl.when(step == 0)
    def _():
        sums_ref[...] = jnp.zeros_like(sums_ref)
        sum_up_ref[...] = jnp.zeros_like(sum_up_ref)

    def add_sum(k, values):
        sums_ref[k : k + 1, :] += jnp.sum(values, 0, keepdims=True)

    add_sum(0, grad * second_normed)
    add_sum(1, grad)
    add_sum(2, grad_ffn.astype(f32))
    for c in range(0, wide, CHUNK):
        at = slice(c, c + CHUNK)
        grad_raised = (nt(grad_ffn, w_d_ref[at, :]) * slope_ref[:, at]).astype(bf)
        grad_raised_ref[:, at] = grad_raised
        sum_up_ref[:, at] += jnp.sum(grad_raised.astype(f32), 0, keepdims=True)
    grad_hidden = nt(grad_raised_ref[...], w_u_ref[...]) + grad_mixed
    add_sum(3, grad_hidden * first_normed)
    add_sum(4, grad_hidden)
    grad_first = normalize_back(grad_hidden * g_first, first_normed, first_inverse)
    grad_first_ref[...] = grad_first
    add_sum(6, jnp.where(second, 0.0, grad_first))
    add_sum(7, jnp.where(second, grad_first, 0.0))
    grad_att = grad_first.astype(bf)
    grad_att_ref[...] = grad_att
    add_sum(5, grad_att.astype(f32))
    grad_ctx_ref[...] = nt(w_o, grad_att).astype(bf)


def ffn(boundary, core, context_t, tokens, out_grad, view, w_u, w_d, vec, v_up, seq_len):
    total, features = tokens.shape
    wide = w_u.shape[1]
    whole = lambda a: pl.BlockSpec(a.shape, lambda i, *_: (0, 0), pipeline_mode=pl.Buffered(1))
    narrow = pl.BlockSpec((ROWS, features), lambda i, *_: (i, 0))
    broad = pl.BlockSpec((ROWS, wide), lambda i, *_: (i, 0))
    turned = pl.BlockSpec((features, ROWS), lambda i, *_: (0, i))
    shape = jax.ShapeDtypeStruct
    return pl.pallas_call(
        lambda *refs: ffn_kernel(*refs, seq_len=seq_len),
        grid_spec=pltpu.PrefetchScalarGridSpec(
            num_scalar_prefetch=2,
            grid=(total // ROWS,),
            in_specs=[turned, narrow, narrow, *weight_view(view, 3, features), whole(w_u), whole(w_d), whole(vec), whole(v_up)],
            out_specs=[
                narrow, narrow, broad, narrow, broad, narrow, narrow, turned,
                pl.BlockSpec((8, features), lambda i, *_: (0, 0)),
                pl.BlockSpec((1, wide), lambda i, *_: (0, 0)),
            ],
            scratch_shapes=[pltpu.VMEM((ROWS, wide), f32)],
        ),
        out_shape=[
            shape((total, features), bf), shape((total, features), bf), shape((total, wide), bf),
            shape((total, features), bf), shape((total, wide), bf), shape((total, features), f32),
            shape((total, features), bf), shape((features, total), bf),
            shape((8, features), f32), shape((1, wide), f32),
        ],
        compiler_params=pltpu.CompilerParams(vmem_limit_bytes=VMEM_LIMIT),
        cost_estimate=pl.CostEstimate(
            flops=2 * total * features * (4 * wide + 2 * features),
            bytes_accessed=2 * (2 * features * wide + 2 * total * wide + 8 * total * features),
            transcendentals=2 * total * wide),
    )(boundary, core, context_t, tokens, out_grad, *view[:2], w_u, w_d, vec, v_up)


def outer_kernel(active_ref, grad_ffn_ref, hidden_ref, grad_raised_ref, out_ref):
    parts, devices, cut, features = out_ref.shape
    step = pl.program_id(0)
    half = pl.num_programs(0) // 2

    @pl.when(step < half)
    def _():
        for f in range(devices):
            at = slice(f * parts * cut, (f + 1) * parts * cut)
            values = tn(active_ref[:, at], grad_ffn_ref[...]).astype(bf)
            for k in range(parts):
                out_ref[k, f] = values[k * cut : (k + 1) * cut, :]

    @pl.when(step >= half)
    def _():
        for k in range(parts):
            values = tn(hidden_ref[...], grad_raised_ref[:, k * features : (k + 1) * features]).astype(bf)
            for f in range(devices):
                out_ref[k, f] = values[f * cut : (f + 1) * cut, :]


def outer(active, grad_ffn, hidden, grad_raised, devices):
    total, features = hidden.shape
    wide = active.shape[1]
    parts, cut = wide // features, features // devices
    blocks = 2
    fixed = lambda a: pl.BlockSpec(a.shape, lambda i: (0, 0), pipeline_mode=pl.Buffered(1))
    return pl.pallas_call(
        outer_kernel,
        grid=(2 * blocks,),
        in_specs=[
            pl.BlockSpec((total, wide // blocks), lambda i: (0, jnp.minimum(i, blocks - 1))), fixed(grad_ffn),
            pl.BlockSpec((total, features // blocks), lambda i: (0, jnp.maximum(i - blocks, 0))), fixed(grad_raised)],
        out_specs=pl.BlockSpec((parts, devices // blocks, cut, features), lambda i: (i // blocks, i % blocks, 0, 0)),
        out_shape=jax.ShapeDtypeStruct((2 * parts, devices, cut, features), bf),
        compiler_params=pltpu.CompilerParams(vmem_limit_bytes=VMEM_LIMIT),
        cost_estimate=pl.CostEstimate(
            flops=4 * total * features * wide, bytes_accessed=4 * wide * (features + total), transcendentals=0),
    )(active, grad_ffn, hidden, grad_raised)


TILE = 16
WAIT_FOR = 2


def swap_core(a):
    n = lax.axis_size("fsdp")
    return lax.ppermute(a, "fsdp", [(i, i ^ 1) for i in range(n)])


def swap_line(a):
    n = lax.axis_size("fsdp")
    groups = [list(range(c, n, 2)) for c in range(2)]
    return lax.all_to_all(a, "fsdp", 0, 0, tiled=True, axis_index_groups=groups)


def along_line(a, step):
    n = lax.axis_size("fsdp")
    return lax.ppermute(a, "fsdp", [(i, i + 2 * step) for i in range(n) if 0 <= i + 2 * step < n])


def swap_rep(a):
    return lax.all_to_all(a, "rep", 0, 0, tiled=True)


def flip_rep(a, bit):
    return lax.ppermute(a, "rep", [(i, i ^ bit) for i in range(lax.axis_size("rep"))])


def after(a, *others):
    return lax.optimization_barrier((a,) + others)[0]


def spread(a, copies):
    return jnp.broadcast_to(a[None], (copies,) + a.shape)


def gather_rep(a):
    reps = lax.axis_size("rep")
    bits = [1 << k for k in range(reps.bit_length() - 1)]
    width = a.shape[-1] // len(bits)
    me = lax.axis_index("rep")
    shares = []
    for k in range(len(bits)):
        share = a[None, ..., k * width : (k + 1) * width]
        order = bits[k:] + bits[:k]
        for bit in order:
            other = flip_rep(share, bit)
            high = (me // bit) % 2 == 1
            share = jnp.concatenate([jnp.where(high, other, share), jnp.where(high, share, other)])
        at = np.zeros(reps, np.int32)
        for place in range(reps):
            rep = sum(bit for i, bit in enumerate(order) if (place >> i) & 1)
            at[rep] = place
        shares.append(jnp.stack([share[int(p)] for p in at]))
    return jnp.concatenate(shares, axis=-1)


def gather_parts(mine, shard, *others):
    places = lax.axis_size("fsdp") // 2
    place = lax.axis_index("fsdp") // 2
    steps = [k for d in range(1, places) for k in (d, -d)]
    seen = {-k: along_line(mine, k) for k in steps}
    near = min(WAIT_FOR, places - 1)
    seen[near], seen[-near], *others = lax.optimization_barrier((seen[near], seen[-near], *others))
    line = jnp.stack([seen[k] for k in range(1 - places, places) if k])
    line = lax.dynamic_slice_in_dim(line, places - 1 - place, places - 1, 0)
    every = gather_rep(line)
    at = jnp.arange(places)[:, None, None, None]
    every = every.swapaxes(0, 1)
    before = jnp.pad(every, ((0, 1), (0, 0), (0, 0), (0, 0)))
    behind = jnp.pad(every, ((1, 0), (0, 0), (0, 0), (0, 0)))
    every = jnp.where(at == place, shard[None], jnp.where(at < place, before, behind))
    other = swap_core(every)
    return every, other, others


def summed_over(a):
    return jnp.sum(a.astype(f32), 0).astype(bf)


def pad_tail(a, rows, columns):
    return jnp.pad(a, [(0, 0)] * (a.ndim - 2) + [(0, rows - a.shape[-2]), (0, columns - a.shape[-1])])


def per_device(
    tokens, lengths, boundary,
    w_query, b_query, w_key, b_key, w_value, b_value, w_out, b_out,
    first_gain, first_shift, w_up, b_up, w_down, b_down,
    second_gain, second_shift, rel_table, type_table, out_grad,
):
    micros, seqs, seq_len, features = tokens.shape
    rows = micros * seqs * seq_len
    heads = features // HEAD_DIM
    fs, reps = lax.axis_size("fsdp"), lax.axis_size("rep")
    places = fs // 2
    cut = w_query.shape[0]
    unit = 4 * cut // reps
    table_cut = rel_table.shape[0] // reps
    up_parts = w_up.shape[1] // features
    vectors = jnp.stack([b_query, b_key, b_value, b_out, first_gain, first_shift, b_down, second_gain,
                         second_shift, type_table[0], type_table[1]] + [b_up[k * cut : (k + 1) * cut] for k in range(up_parts)])
    vector_count = vectors.shape[0]
    vector_rows = -(-vector_count // TILE) * TILE
    vectors = pad_tail(vectors, vector_rows, features)
    shard = jnp.concatenate([
        jnp.stack([w_query, w_key, w_value, w_out]).reshape(reps, unit, features),
        rel_table.reshape(reps, table_cut, features),
        spread(vectors, reps)], axis=1)
    mine = lax.dynamic_index_in_dim(shard, lax.axis_index("rep"), 0, keepdims=False)
    own, other, (w_up, w_down) = gather_parts(mine, shard, w_up, w_down)
    w_u = lax.all_gather(w_up, "fsdp", axis=0, tiled=True)
    w_d = lax.all_gather(w_down, "fsdp", axis=0, tiled=True)
    direct = unit if unit == cut and cut % TILE == 0 and table_cut % TILE == 0 else 0
    part = unit + table_cut + vector_rows
    core = lax.axis_index("fsdp") % 2
    first = jnp.stack([jnp.where(core == 0, own, other), jnp.where(core == 0, other, own)], axis=1)
    if direct:
        view = (own, other, cut, own, other, (places, reps, table_cut, features), (0, 0, unit // table_cut, 0))
    else:
        four = first[:, :, :, :unit].reshape(fs, 4, reps // 4, unit, features).transpose(1, 0, 2, 3, 4)
        four = four.reshape(1, 4, features, features)
        rel = first[:, :, :, unit : unit + table_cut].reshape(1, 1, -1, features)
        view = (four, four, features, rel, rel, rel.shape, (0,) * 4)
    vector_at = slice(unit + table_cut, unit + table_cut + vector_count)
    wide = [a[:, 0, vector_at, :cut] for a in (own, other)]
    wide = jnp.stack([jnp.where(core == 0, *wide), jnp.where(core == 0, *wide[::-1])], axis=1)
    wide = wide.reshape(fs, vector_count, cut)
    core = core.reshape(1)
    wide = wide.transpose(1, 0, 2).astype(f32)
    v_up = wide[vector_count - up_parts :].transpose(1, 0, 2).reshape(1, -1)
    wide = wide.reshape(vector_count, features)

    offsets = np.clip(np.arange(2 * seq_len) - (seq_len - 1), 1 - seq_len, seq_len - 1)
    pick = pick_rows(offsets)
    pick_back = pick_rows(-offsets)
    flat_bound, flat_lengths = boundary.reshape(-1), lengths.reshape(-1)
    flat_tokens, flat_grad = tokens.reshape(rows, features), out_grad.reshape(rows, features)
    queries, keys, values, key_rows, query_rows, key_back_t, query_t, summed_low = project(
        flat_bound, core, flat_tokens, view, jnp.asarray(pick, bf), jnp.asarray(pick.T, bf), jnp.asarray(pick_back.T, bf),
        wide, wide[9:11], seq_len)
    context_t, probs, inverse_total = attn_fwd(
        queries, keys, values, key_back_t, query_t, flat_lengths, heads)
    (layer_out, hidden_low, active, grad_ffn, grad_raised, grad_first, grad_attended, grad_context_t,
     sums, sum_up) = ffn(flat_bound, core, context_t, flat_tokens, flat_grad, view, w_u, w_d, wide, v_up, seq_len)
    d_ffn = outer(active, grad_ffn, hidden_low, grad_raised, fs)
    early = lax.psum_scatter(d_ffn.reshape(-1, features, features), "fsdp", scatter_dimension=1, tiled=True)
    d_query, d_key, d_value, key_off, query_off = attn_bwd(
        queries, keys, values, grad_context_t, probs, inverse_total, key_rows, query_rows)
    made = unproject(
        flat_bound, core, summed_low, d_query, d_key, d_value, key_off, query_off, view,
        jnp.asarray(pick.T, bf), context_t, grad_attended, sums, sum_up, seq_len, direct,
        (reps, places, part, features))
    tokens_grad = token_grads(core, d_query, d_key, d_value, view, grad_first)
    if direct:
        keep, give = made
    else:
        four, d_rel, small = made
        four = four.reshape(4, places, 2, reps // 4, unit, features).transpose(0, 3, 1, 2, 4, 5)
        small = jnp.broadcast_to(small.astype(bf), (reps, places, 2) + small.shape)
        last = jnp.concatenate([
            four.reshape(reps, places, 2, unit, features),
            d_rel.reshape(places, 2, reps, table_cut, features).transpose(2, 0, 1, 3, 4), small], axis=3)
        keep = lax.dynamic_index_in_dim(last, core[0], 2, keepdims=False)
        give = lax.dynamic_index_in_dim(last, 1 - core[0], 2, keepdims=False)
    last = (keep.astype(f32) + swap_core(give).astype(f32)).astype(bf)
    early = lax.psum_scatter(early.reshape(-1, features), "rep", scatter_dimension=0, tiled=True)
    last = summed_over(swap_rep(last))
    early = after(early, last)
    early = lax.all_gather(early, "rep", axis=0, tiled=True)
    last = summed_over(swap_line(last))
    small = last[unit + table_cut : unit + table_cut + vector_count].astype(f32)
    small = lax.dynamic_slice_in_dim(small[: vector_count - up_parts], lax.axis_index("fsdp") * cut, cut, 1)
    d_b_up = last[unit + table_cut + vector_count - up_parts : unit + table_cut + vector_count].astype(f32)
    d_b_up = lax.dynamic_slice_in_dim(d_b_up.reshape(-1), lax.axis_index("fsdp") * up_parts * cut, up_parts * cut, 0)
    both = swap_rep(spread(last[: unit + table_cut], reps)).astype(f32)
    four = both[:, :unit].reshape(4, cut, features)
    s_q, s_k, s_v, s_o = four[0], four[1], four[2], four[3]
    s_rel = both[:, unit:].reshape(-1, features)
    (d_b_query, d_b_key, d_b_value, d_b_out, d_first_gain, d_first_shift, d_b_down,
     d_second_gain, d_second_shift, d_type_zero, d_type_one) = [
        small[k] for k in range(vector_count - up_parts)]
    s_down = early[: w_down.shape[0]].astype(f32)
    s_up = early[w_down.shape[0] :].reshape(up_parts, cut, features).transpose(1, 0, 2)
    s_up = s_up.reshape(cut, -1).astype(f32)
    return (
        layer_out.reshape(tokens.shape), tokens_grad.reshape(tokens.shape),
        s_q, d_b_query, s_k, d_b_key, s_v, d_b_value, s_o, d_b_out,
        d_first_gain, d_first_shift, s_up, d_b_up, s_down, d_b_down,
        d_second_gain, d_second_shift, s_rel, jnp.stack([d_type_zero, d_type_one]),
    )


def solution(mesh):
    seq = P(None, ("rep", "fsdp"), None, None)
    flat = P(None, ("rep", "fsdp"))
    mat, vec = P("fsdp", None), P("fsdp")
    weights = (mat, vec, mat, vec, mat, vec, mat, vec, vec, vec, mat, vec, mat, vec, vec, vec, mat,
               P(None, "fsdp"))
    return jax.shard_map(
        per_device,
        mesh=mesh,
        in_specs=(seq, flat, flat) + weights + (seq,),
        out_specs=(seq, seq) + weights,
        check_vma=False,
    )
```

```python
import math

import jax
import jax.numpy as jnp
import numpy as np
from jax import lax
from jax.experimental import pallas as pl
from jax.experimental.pallas import tpu as pltpu
from jax.sharding import PartitionSpec as P

BUCKETS = 256
MAX_POS = 512
NORM_EPS = 1e-07
VMEM_LIMIT = 62 * 1024 * 1024

HEAD_DIM=64
MASKED=-1e30
f32=jnp.float32; bf=jnp.bfloat16
BLK=128
LOG2E=math.log2(math.e)

def nn(a,b): return lax.dot_general(a,b,(((1,),(0,)),((),())),preferred_element_type=f32)
def nt(a,b): return lax.dot_general(a,b,(((1,),(1,)),((),())),preferred_element_type=f32)

def eye(rows, flip=False):
    r=lax.broadcasted_iota(jnp.int32,(rows,rows),0)
    c=lax.broadcasted_iota(jnp.int32,(rows,rows),1)
    return jnp.where((r+c==rows-1) if flip else (r==c),1.0,0.0).astype(bf)

def attn_fwd_kernel(len_ref,q_ref,k_ref,v_ref,pkrT_ref,pqT_ref,ctxT_ref,p_ref,linv_ref,c_scr,s_scr):
    S=q_ref.shape[0]
    nb=S//BLK
    W=S+BLK
    m=pl.program_id(1)
    length=len_ref[m]
    scale=LOG2E/math.sqrt(3*HEAD_DIM)
    q=q_ref[...]; k=k_ref[...]
    pqT=pqT_ref[...]
    vT=v_ref[...].T; qT=q.T
    row_h=lax.broadcasted_iota(jnp.int32,(2*HEAD_DIM,S),0)
    lane_s=lax.broadcasted_iota(jnp.int32,(S,2*HEAD_DIM),1)
    row_s=lax.broadcasted_iota(jnp.int32,(S,2*HEAD_DIM),0)
    row_t=lax.broadcasted_iota(jnp.int32,(2*HEAD_DIM,2*S),0)
    bias=jnp.where(row_s<length,0.0,MASKED).astype(bf)
    zero=jnp.zeros((),bf)
    pos=lax.broadcasted_iota(jnp.int32,(1,S),1)
    for h in range(2):
        mine=(lane_s<HEAD_DIM) if h==0 else (lane_s>=HEAD_DIM)
        spare=HEAD_DIM if h==0 else 0
        qh=jnp.where(mine,q,zero)
        kb=jnp.where(mine,k,jnp.where(lane_s==spare,bias,zero))
        pqh=jnp.where(row_t==spare,jnp.ones((),bf),pqT)
        qTh=jnp.where((row_h<HEAD_DIM) if h==0 else (row_h>=HEAD_DIM),qT,zero)
        for b in range(nb):
            st=(nb-1-b)*BLK
            c=nn(qh[b*BLK:(b+1)*BLK],pkrT_ref[:,st:st+W]).astype(bf)
            c_scr[h,b*BLK:(b+1)*BLK,:]=pltpu.roll(c,S+1,1,stride=1,stride_axis=0)[:,:S]
        top=None
        for b in range(nb):
            st=(nb-1-b)*BLK
            js=slice(b*BLK,(b+1)*BLK)
            d=nn(kb[js],pqh[:,st:st+W]).astype(bf)
            d=pltpu.roll(d,S+1,1,stride=1,stride_axis=0)[:,:S]
            s=nn(k[js],qTh)+(c_scr[h,:,js].T.astype(f32)+d.astype(f32))
            s_scr[h,js,:]=s
            t=jnp.max(s,axis=0,keepdims=True)
            top=t if top is None else jnp.maximum(top,t)
        top=top*scale
        tot=None
        for b in range(nb):
            js=slice(b*BLK,(b+1)*BLK)
            p=jnp.exp2(s_scr[h,js,:]*scale-top).astype(bf)
            t=jnp.sum(p.astype(f32),axis=0,keepdims=True)
            tot=t if tot is None else tot+t
            p_ref[0,h,js,:]=p
        linv=jnp.where(pos<length,1.0/tot,0.0)
        linv_ref[0,0,h:h+1,:]=linv
        ctx=nn(vT[h*HEAD_DIM:(h+1)*HEAD_DIM,:],p_ref[0,h])*linv
        ctxT_ref[h*HEAD_DIM:(h+1)*HEAD_DIM,:]=ctx.astype(bf)

def attn_fwd(q,k,v,pkr,pq,lengths,heads):
    M=lengths.shape[0]; D=heads*HEAD_DIM
    S=pq.shape[1]//2
    NP=heads//2; L=2*HEAD_DIM
    grid=(NP,M)
    return pl.pallas_call(
        attn_fwd_kernel,
        grid_spec=pltpu.PrefetchScalarGridSpec(
            num_scalar_prefetch=1,grid=grid,
            in_specs=[
                pl.BlockSpec((S,L),lambda p,m,_:(m,p)),
                pl.BlockSpec((S,L),lambda p,m,_:(m,p)),
                pl.BlockSpec((S,L),lambda p,m,_:(m,p)),
                pl.BlockSpec((L,2*S),lambda p,m,_:(p,0)),
                pl.BlockSpec((L,2*S),lambda p,m,_:(p,0)),
            ],
            out_specs=[
                pl.BlockSpec((L,S),lambda p,m,_:(p,m)),
                pl.BlockSpec((1,2,S,S),lambda p,m,_:(m,p,0,0)),
                pl.BlockSpec((1,1,2,S),lambda p,m,_:(m,p,0,0)),
            ],
            scratch_shapes=[pltpu.VMEM((2,S,S),bf),pltpu.VMEM((2,S,S),f32)],
        ),
        out_shape=[jax.ShapeDtypeStruct((D,M*S),bf),jax.ShapeDtypeStruct((M,heads,S,S),bf),jax.ShapeDtypeStruct((M,NP,2,S),f32)],
        compiler_params=pltpu.CompilerParams(vmem_limit_bytes=VMEM_LIMIT),
        cost_estimate=pl.CostEstimate(flops=int(2*M*heads*S*S*64*12),bytes_accessed=int(M*heads*S*S*2),transcendentals=M*heads*S*S),
    )(lengths,q,k,v,pkr,pq)

def attn_bwd_kernel(q_ref,k_ref,v_ref,dcT_ref,p_ref,linv_ref,pk_ref,pq_ref,dq_ref,dk_ref,dv_ref,ko_out,qo_out,ds_scr,p_scr,t_scr,ko_ref,qo_ref):
    S=q_ref.shape[0]
    nb=S//BLK
    W=S+BLK
    m=pl.program_id(1)
    scale=1.0/math.sqrt(3*HEAD_DIM)
    zero=jnp.zeros((),bf)
    flip=eye(BLK,True)
    q=q_ref[...]
    def reverse(x):
        return jnp.concatenate([nn(flip,x[(nb-1-b)*BLK:(nb-b)*BLK]).astype(bf) for b in range(nb)],axis=0)
    kr=reverse(k_ref[...]); vr=reverse(v_ref[...])
    qT=q.T; krT=kr.T
    lane_s=lax.broadcasted_iota(jnp.int32,(S,2*HEAD_DIM),1)
    lane_t=lax.broadcasted_iota(jnp.int32,(2*S,2*HEAD_DIM),1)
    pad=jnp.zeros((BLK,BLK),bf)
    @pl.when(m==0)
    def _():
        ko_ref[...]=jnp.zeros_like(ko_ref)
        qo_ref[...]=jnp.zeros_like(qo_ref)
    dq=[None]*nb; dk=[None]*nb; dv=None
    zrow=jnp.zeros((HEAD_DIM,S),bf)
    for h in range(2):
        hs=slice(h*HEAD_DIM,(h+1)*HEAD_DIM)
        mine=(lane_s<HEAD_DIM) if h==0 else (lane_s>=HEAD_DIM)
        mine_t=(lane_t<HEAD_DIM) if h==0 else (lane_t>=HEAD_DIM)
        qh=jnp.where(mine,q,zero); krh=jnp.where(mine,kr,zero)
        pkh=jnp.where(mine_t,pk_ref[...],zero); pqh=jnp.where(mine_t,pq_ref[...],zero)
        linv=linv_ref[0,0,h:h+1,:]
        dc=dcT_ref[hs,:].astype(f32)*linv
        dcl=dc.astype(bf); dcs=(dc*scale).astype(bf)
        def wide(x): return jnp.concatenate([x,zrow] if h==0 else [zrow,x],axis=0)
        t=nt(p_ref[0,h],wide(dcl))
        dv=t if dv is None else dv+t
        dcw=wide(dcs)
        delta=None
        dp=nn(vr,dcw)
        for b in range(nb):
            js=slice(b*BLK,(b+1)*BLK)
            p=nn(flip,p_ref[0,h,(nb-1-b)*BLK:(nb-b)*BLK,:])
            t=p*dp[js]
            p_scr[h,js,:]=p
            t_scr[h,js,:]=t
            t=jnp.sum(t,axis=0,keepdims=True)
            delta=t if delta is None else delta+t
        delta=delta*linv
        for b in range(nb):
            js=slice(b*BLK,(b+1)*BLK)
            ds=(t_scr[h,js,:]-p_scr[h,js,:]*delta).astype(bf)
            ds_scr[h,js,:]=ds
            far=pltpu.roll(jnp.concatenate([ds,pad],axis=1),0,1,stride=1,stride_axis=0)
            st=b*BLK
            t=nn(ds,qh)+nn(far,pqh[st:st+W])
            dk[b]=t if dk[b] is None else dk[b]+t
            qo_ref[hs,st:st+W]+=nn(krT[hs,js],far)
        for b in range(nb):
            js=slice(b*BLK,(b+1)*BLK)
            ds=ds_scr[h,:,js].T
            near=pltpu.roll(jnp.concatenate([ds,pad],axis=1),0,1,stride=1,stride_axis=0)
            st=b*BLK
            t=nn(ds,krh)+nn(near,pkh[st:st+W])
            dq[b]=t if dq[b] is None else dq[b]+t
            ko_ref[hs,st:st+W]+=nn(qT[hs,js],near)
    @pl.when(m==pl.num_programs(1)-1)
    def _():
        ko_out[...]=ko_ref[...].astype(bf)
        qo_out[...]=qo_ref[...].astype(bf)
    dv_ref[...]=dv.astype(bf)
    for b in range(nb):
        dq_ref[b*BLK:(b+1)*BLK,:]=dq[b].astype(bf)
        dk_ref[(nb-1-b)*BLK:(nb-b)*BLK,:]=nn(flip,dk[b].astype(bf)).astype(bf)

def attn_bwd(q,k,v,dcT,p,linv,pk,pq):
    M,heads,S,_=p.shape; D=heads*HEAD_DIM
    NP=heads//2; L=2*HEAD_DIM
    tok=lambda off: pl.BlockSpec((S,L),lambda p,m:(m,off+p))
    colT=pl.BlockSpec((L,S),lambda p,m:(p,m))
    tab=pl.BlockSpec((2*S,L),lambda p,m:(0,p))
    return pl.pallas_call(
        attn_bwd_kernel,
        grid=(NP,M),
        in_specs=[tok(0),tok(0),tok(0),colT,
            pl.BlockSpec((1,2,S,S),lambda p,m:(m,p,0,0)),
            pl.BlockSpec((1,1,2,S),lambda p,m:(m,p,0,0)),
            tab,tab],
        out_specs=[tok(0),tok(0),tok(0),pl.BlockSpec((L,2*S),lambda p,m:(p,0)),pl.BlockSpec((L,2*S),lambda p,m:(p,0))],
        out_shape=[jax.ShapeDtypeStruct((M*S,D),bf)]*3+[jax.ShapeDtypeStruct((D,2*S),bf)]*2,
        scratch_shapes=[pltpu.VMEM((2,S,S),bf),pltpu.VMEM((2,S,S),f32),pltpu.VMEM((2,S,S),f32),pltpu.VMEM((L,2*S),f32),pltpu.VMEM((L,2*S),f32)],
        compiler_params=pltpu.CompilerParams(vmem_limit_bytes=VMEM_LIMIT),
        cost_estimate=pl.CostEstimate(flops=int(2*M*heads*S*S*64*24),bytes_accessed=int(M*heads*S*S*2),transcendentals=0),
    )(q,k,v,dcT,p,linv,pk,pq)


def bucket_index(offset_of):
    middle = BUCKETS // 2
    sign_of = np.sign(offset_of)
    magnitude = np.where(
        (offset_of < middle) & (offset_of > -middle), middle - 1, np.abs(offset_of)
    )
    log_pos = (
        np.ceil(np.log(magnitude / middle) / np.log((MAX_POS - 1) / middle) * (middle - 1)) + middle
    )
    bucket = np.where(magnitude <= middle, offset_of, log_pos * sign_of)
    return np.clip(bucket + BUCKETS, 0, 2 * BUCKETS - 1)


def pick_rows(offsets):
    return (bucket_index(offsets)[:, None] == np.arange(2 * BUCKETS)[None, :]).astype(np.float32)


def tn(a, b):
    return lax.dot_general(a, b, (((0,), (0,)), ((), ())), preferred_element_type=f32)

COLUMNS = 256


def second_rows(bound_ref, rows, seq_len):
    at = lax.broadcasted_iota(jnp.int32, (rows, 1), 0)
    second = at < 0
    for m in range(rows // seq_len):
        second = second | ((at >= m * seq_len + bound_ref[m]) & (at < (m + 1) * seq_len))
    return second


def project_kernel(
    bound_ref, core_ref, tokens_ref, w_q_ref, w_q2_ref, w_k_ref, w_k2_ref, w_v_ref, w_v2_ref, rel_ref, rel2_ref,
    pick_ref, pick_t_ref, pick_back_t_ref, vec_ref,
    type_ref, q_ref, k_ref, v_ref, key_ref, query_ref, key_back_ref, query_t_ref, low_ref, *, seq_len,
):
    rows = tokens_ref.shape[0]

    @pl.when(pl.program_id(0) == 0)
    def _():
        second = second_rows(bound_ref, rows, seq_len)
        low_ref[...] = (
            tokens_ref[...].astype(f32) + jnp.where(second, type_ref[1:2, :], type_ref[0:1, :])
        ).astype(bf)

    low = low_ref[...]
    first = core_ref[0] == 0
    rel = in_order(rel_ref, rel2_ref, first, pick_ref.shape[1])
    features = tokens_ref.shape[1]
    w_q = in_order(w_q_ref, w_q2_ref, first, features)
    w_k = in_order(w_k_ref, w_k2_ref, first, features)
    w_v = in_order(w_v_ref, w_v2_ref, first, features)
    b_q, b_k = vec_ref[0:1, :], vec_ref[1:2, :]
    q_ref[...] = (nn(low, w_q) + b_q).astype(bf)
    k_ref[...] = (nn(low, w_k) + b_k).astype(bf)
    v_ref[...] = (nn(low, w_v) + vec_ref[2:3, :]).astype(bf)
    pos_query = (nn(rel, w_q) + b_q).astype(bf)
    pos_key = (nn(rel, w_k) + b_k).astype(bf)
    query_ref[...] = nn(pick_ref[...], pos_query).astype(bf)
    key_ref[...] = nn(pick_ref[...], pos_key).astype(bf)
    key_back_ref[...] = tn(pos_key, pick_back_t_ref[...]).astype(bf)
    query_t_ref[...] = tn(pos_query, pick_t_ref[...]).astype(bf)


def weight_view(view, g, columns):
    spec = pl.BlockSpec((view[0].shape[0], 1, view[2], columns), lambda i, *_: (0, g, 0, i if columns == COLUMNS else 0),
                        pipeline_mode=None if columns == COLUMNS else pl.Buffered(1))
    return [spec, spec]


def table_view(view):
    spec = pl.BlockSpec(view[5], lambda i, *_: view[6], pipeline_mode=pl.Buffered(1))
    return [spec, spec]


def in_order(own_ref, other_ref, first, rows):
    own = own_ref[...]
    columns = own.shape[-1]
    if own.size == rows * columns:
        return own.reshape(rows, columns)
    other = other_ref[...]
    both = jnp.stack([jnp.where(first, own, other), jnp.where(first, other, own)], axis=1)
    return both.reshape(rows, columns)


def project(boundary, core, tokens, view, pick, pick_t, pick_back_t, vec, types, seq_len):
    total, features = tokens.shape
    table_rows = pick.shape[1]
    whole = lambda a: pl.BlockSpec(a.shape, lambda i, *_: (0,) * a.ndim, pipeline_mode=pl.Buffered(1))
    weight = lambda g: weight_view(view, g, COLUMNS)
    columns = lambda rows: pl.BlockSpec((rows, COLUMNS), lambda i, *_: (0, i))
    shape = jax.ShapeDtypeStruct
    offsets = pick.shape[0]
    return pl.pallas_call(
        lambda *refs: project_kernel(*refs, seq_len=seq_len),
        grid_spec=pltpu.PrefetchScalarGridSpec(
            num_scalar_prefetch=2,
            grid=(features // COLUMNS,),
            in_specs=[whole(tokens), *weight(0), *weight(1), *weight(2), *table_view(view), whole(pick),
                      whole(pick_t), whole(pick_back_t), columns(vec.shape[0]), whole(types)],
            out_specs=[columns(total)] * 3 + [columns(offsets)] * 2
            + [pl.BlockSpec((COLUMNS, offsets), lambda i, *_: (i, 0))] * 2
            + [pl.BlockSpec((total, features), lambda i, *_: (0, 0))],
        ),
        out_shape=[shape((total, features), bf)] * 3 + [shape((offsets, features), bf)] * 2
        + [shape((features, offsets), bf)] * 2
        + [shape((total, features), bf)],
        compiler_params=pltpu.CompilerParams(vmem_limit_bytes=VMEM_LIMIT),
        cost_estimate=pl.CostEstimate(
            flops=2 * features * features * (3 * total + 2 * table_rows) + 6 * offsets * features * table_rows,
            bytes_accessed=2 * features * (3 * features + 5 * total + 3 * offsets), transcendentals=0),
    )(boundary, core, tokens, *(view[:2] * 3), *view[3:5], pick, pick_t, pick_back_t, vec, types)


def unproject_kernel(
    bound_ref, core_ref, low_ref, dq_ref, dk_ref, dv_ref, key_off_ref, query_off_ref, w_q_ref, w_q2_ref,
    w_k_ref, w_k2_ref, w_v_ref, w_v2_ref, rel_ref, rel2_ref, pick_t_ref, context_ref, grad_att_ref, sums_ref, sum_up_ref,
    *refs, seq_len, direct,
):
    if direct:
        keep_ref, give_ref, rel_sum_ref, small_ref = refs
    else:
        dw_ref, drel_ref, small_ref, rel_sum_ref = refs
    step = pl.program_id(0)
    rows, features = low_ref.shape
    first = core_ref[0] == 0

    @pl.when(step == 0)
    def _():
        rel_sum_ref[...] = jnp.zeros_like(rel_sum_ref)
        small_ref[...] = jnp.zeros_like(small_ref)
        small_ref[9:11, :] = sums_ref[6:8, :]

    low, rel = low_ref[...], in_order(rel_ref, rel2_ref, first, pick_t_ref.shape[0])
    w_q = in_order(w_q_ref, w_q2_ref, first, features)
    w_k = in_order(w_k_ref, w_k2_ref, first, features)
    w_v = in_order(w_v_ref, w_v2_ref, first, features)
    dq, dk, dv = dq_ref[...], dk_ref[...], dv_ref[...]
    columns = pl.ds(pl.multiple_of(step * COLUMNS, COLUMNS), COLUMNS)

    def put(at, rows_at, values):
        if direct:
            _, places, part, _ = keep_ref.shape
            values = values.astype(bf).reshape(places, 2, -1, values.shape[-1])
            keep_ref[at, :, rows_at, columns] = jnp.where(first, values[:, 0], values[:, 1])
            give_ref[at, :, rows_at, columns] = jnp.where(first, values[:, 1], values[:, 0])
        else:
            dw_ref[at] = values.astype(bf)

    unit = direct
    pos_query = nt(pick_t_ref[...], query_off_ref[...])
    pos_key = nt(pick_t_ref[...], key_off_ref[...])
    low_query, low_key = pos_query.astype(bf), pos_key.astype(bf)
    put(0, slice(0, unit), tn(low, dq) + tn(rel, low_query))
    put(1, slice(0, unit), tn(low, dk) + tn(rel, low_key))
    put(2, slice(0, unit), tn(low, dv))
    put(3, slice(0, unit), nn(context_ref[...], grad_att_ref[...]))
    total = lambda a: jnp.sum(a.astype(f32), 0, keepdims=True)
    small_ref[0:1, columns] = total(dq) + total(pos_query)
    small_ref[1:2, columns] = total(dk) + total(pos_key)
    small_ref[2:3, columns] = total(dv)
    second = second_rows(bound_ref, rows, seq_len)
    for values, weight in ((dq, w_q), (dk, w_k), (dv, w_v)):
        wide = values.astype(f32)
        row = lax.broadcasted_iota(jnp.int32, (16, wide.shape[1]), 0)
        parts = jnp.where(row == 0, total(jnp.where(second, 0.0, wide)), 0.0)
        parts = jnp.where(row == 1, total(jnp.where(second, wide, 0.0)), parts)
        high = parts.astype(bf)
        product = nt(high, weight) + nt((parts - high.astype(f32)).astype(bf), weight)
        small_ref[9:11, :] += product[0:2]
    rel_sum_ref[...] += nt(low_key, w_k) + nt(low_query, w_q)

    @pl.when(step == pl.num_programs(0) - 1)
    def _():
        for at, k in ((3, 5), (4, 3), (5, 4), (6, 2), (7, 0), (8, 1)):
            small_ref[at : at + 1, :] = sums_ref[k : k + 1, :]
        for k in range(sum_up_ref.shape[1] // features):
            small_ref[11 + k : 12 + k, :] = sum_up_ref[:, k * features : (k + 1) * features]
        if direct:
            reps, places, part, _ = keep_ref.shape
            table = rel_sum_ref[...].astype(bf).reshape(places, 2, reps, -1, features)
            small = small_ref[...].astype(bf)
            end = unit + table.shape[3]
            for r in range(reps):
                keep_ref[r, :, unit:end, :] = jnp.where(first, table[:, 0, r], table[:, 1, r])
                give_ref[r, :, unit:end, :] = jnp.where(first, table[:, 1, r], table[:, 0, r])
                for z in range(places):
                    keep_ref[r, z, end:part, :] = small
                    give_ref[r, z, end:part, :] = small
        else:
            drel_ref[...] = rel_sum_ref[...].astype(bf)


def unproject(boundary, core, low, dq, dk, dv, key_off, query_off, view, pick_t, context_t, grad_att,
              sums, sum_up, seq_len, direct, parts):
    total, features = low.shape
    table_rows = pick_t.shape[0]
    whole = lambda a: pl.BlockSpec(a.shape, lambda i, *_: (0,) * a.ndim, pipeline_mode=pl.Buffered(1))
    weight = lambda g: weight_view(view, g, COLUMNS)
    columns = lambda rows: pl.BlockSpec((rows, COLUMNS), lambda i, *_: (0, i))
    turned = pl.BlockSpec((COLUMNS, key_off.shape[1]), lambda i, *_: (i, 0))
    fixed = lambda s: pl.BlockSpec(s, lambda i, *_: (0,) * len(s))
    shape = jax.ShapeDtypeStruct
    small = (16, features)
    scratch = [pltpu.VMEM((table_rows, features), f32)]
    if direct:
        out_specs = [fixed(parts), fixed(parts)]
        out_shape = [shape(parts, bf), shape(parts, bf)]
        scratch.append(pltpu.VMEM(small, f32))
    else:
        out_specs = [pl.BlockSpec((4, features, COLUMNS), lambda i, *_: (0, 0, i)), fixed((table_rows, features)),
                     fixed(small)]
        out_shape = [shape((4, features, features), bf), shape((table_rows, features), bf), shape(small, f32)]
    return pl.pallas_call(
        lambda *refs: unproject_kernel(*refs, seq_len=seq_len, direct=direct),
        grid_spec=pltpu.PrefetchScalarGridSpec(
            num_scalar_prefetch=2,
            grid=(features // COLUMNS,),
            in_specs=[whole(low), columns(total), columns(total), columns(total), turned, turned,
                      *weight(0), *weight(1), *weight(2), *table_view(view), whole(pick_t),
                      whole(context_t), columns(total), whole(sums), whole(sum_up)],
            out_specs=out_specs,
            scratch_shapes=scratch,
        ),
        out_shape=out_shape,
        compiler_params=pltpu.CompilerParams(vmem_limit_bytes=VMEM_LIMIT),
        cost_estimate=pl.CostEstimate(
            flops=2 * features * features * (4 * total + 4 * table_rows) + 8 * total * features * table_rows,
            bytes_accessed=2 * features * (7 * features + 10 * total), transcendentals=0),
    )(boundary, core, low, dq, dk, dv, key_off, query_off, *(view[:2] * 3), *view[3:5], pick_t,
      context_t, grad_att, sums, sum_up)


def token_kernel(core_ref, dq_ref, dk_ref, dv_ref, w_q_ref, w_q2_ref, w_k_ref, w_k2_ref, w_v_ref, w_v2_ref,
                 grad_first_ref, grad_ref):
    first, features = core_ref[0] == 0, dq_ref.shape[1]
    grad_ref[...] = (
        nt(dq_ref[...], in_order(w_q_ref, w_q2_ref, first, features))
        + nt(dk_ref[...], in_order(w_k_ref, w_k2_ref, first, features))
        + nt(dv_ref[...], in_order(w_v_ref, w_v2_ref, first, features)) + grad_first_ref[...]).astype(bf)


def token_grads(core, dq, dk, dv, view, grad_first):
    total, features = dq.shape
    rows = pl.BlockSpec((total // 2, features), lambda i, *_: (i, 0))
    weights = [spec for g in range(3) for spec in weight_view(view, g, features)]
    return pl.pallas_call(
        token_kernel,
        grid_spec=pltpu.PrefetchScalarGridSpec(
            num_scalar_prefetch=1, grid=(2,), in_specs=[rows, rows, rows, *weights, rows], out_specs=rows),
        out_shape=jax.ShapeDtypeStruct((total, features), bf),
        compiler_params=pltpu.CompilerParams(vmem_limit_bytes=VMEM_LIMIT),
        cost_estimate=pl.CostEstimate(
            flops=6 * total * features * features, bytes_accessed=2 * features * (6 * total + 3 * features),
            transcendentals=0),
    )(core, dq, dk, dv, *(view[:2] * 3), grad_first)


ROWS = 256
CHUNK = 512


def normalize(values):
    centred = values - jnp.mean(values, -1, keepdims=True)
    inverse = lax.rsqrt(jnp.mean(centred * centred, -1, keepdims=True) + NORM_EPS)
    return centred * inverse, inverse


def normalize_back(grad, normed, inverse):
    return inverse * (
        grad
        - jnp.mean(grad, -1, keepdims=True)
        - normed * jnp.mean(grad * normed, -1, keepdims=True)
    )


def ffn_kernel(
    bound_ref, core_ref, context_ref, tokens_ref, grad_ref, w_o_ref, w_o2_ref, w_u_ref, w_d_ref, vec_ref, v_up_ref,
    out_ref, hidden_ref, active_ref, grad_ffn_ref, grad_raised_ref, grad_first_ref, grad_att_ref,
    grad_ctx_ref, sums_ref, sum_up_ref, slope_ref, *, seq_len,
):
    step = pl.program_id(0)
    rows = tokens_ref.shape[0]
    wide = w_u_ref.shape[1]
    vec = lambda k: vec_ref[k : k + 1, :]
    w_o = in_order(w_o_ref, w_o2_ref, core_ref[0] == 0, tokens_ref.shape[1])
    v_out, g_first, s_first, v_down, g_second, s_second = [vec(k) for k in range(3, 9)]
    seq = step * rows // seq_len
    pos = step * rows - seq * seq_len + lax.broadcasted_iota(jnp.int32, (rows, 1), 0)
    second = pos >= bound_ref[seq]
    summed = tokens_ref[...].astype(f32) + jnp.where(second, vec(10), vec(9))
    first_normed, first_inverse = normalize(summed + tn(context_ref[...], w_o) + v_out)
    hidden = first_normed * g_first + s_first
    hidden_low = hidden.astype(bf)
    hidden_ref[...] = hidden_low
    for c in range(0, wide, CHUNK):
        at = slice(c, c + CHUNK)
        raised = nn(hidden_low, w_u_ref[:, at]) + v_up_ref[:, at]
        cumulative = 0.5 + 0.5 * lax.erf(raised * (1.0 / math.sqrt(2.0)))
        active_ref[:, at] = (raised * cumulative).astype(bf)
        density = jnp.exp(-0.5 * raised * raised) * (1.0 / math.sqrt(2.0 * math.pi))
        slope_ref[:, at] = cumulative + raised * density
    second_normed, second_inverse = normalize(hidden + nn(active_ref[...], w_d_ref[...]) + v_down)
    out_ref[...] = (second_normed * g_second + s_second).astype(bf)
    grad = grad_ref[...].astype(f32)
    grad_mixed = normalize_back(grad * g_second, second_normed, second_inverse)
    grad_ffn = grad_mixed.astype(bf)
    grad_ffn_ref[...] = grad_ffn

    @pl.when(step == 0)
    def _():
        sums_ref[...] = jnp.zeros_like(sums_ref)
        sum_up_ref[...] = jnp.zeros_like(sum_up_ref)

    def add_sum(k, values):
        sums_ref[k : k + 1, :] += jnp.sum(values, 0, keepdims=True)

    add_sum(0, grad * second_normed)
    add_sum(1, grad)
    add_sum(2, grad_ffn.astype(f32))
    for c in range(0, wide, CHUNK):
        at = slice(c, c + CHUNK)
        grad_raised = (nt(grad_ffn, w_d_ref[at, :]) * slope_ref[:, at]).astype(bf)
        grad_raised_ref[:, at] = grad_raised
        sum_up_ref[:, at] += jnp.sum(grad_raised.astype(f32), 0, keepdims=True)
    grad_hidden = nt(grad_raised_ref[...], w_u_ref[...]) + grad_mixed
    add_sum(3, grad_hidden * first_normed)
    add_sum(4, grad_hidden)
    grad_first = normalize_back(grad_hidden * g_first, first_normed, first_inverse)
    grad_first_ref[...] = grad_first
    add_sum(6, jnp.where(second, 0.0, grad_first))
    add_sum(7, jnp.where(second, grad_first, 0.0))
    grad_att = grad_first.astype(bf)
    grad_att_ref[...] = grad_att
    add_sum(5, grad_att.astype(f32))
    grad_ctx_ref[...] = nt(w_o, grad_att).astype(bf)


def ffn(boundary, core, context_t, tokens, out_grad, view, w_u, w_d, vec, v_up, seq_len):
    total, features = tokens.shape
    wide = w_u.shape[1]
    whole = lambda a: pl.BlockSpec(a.shape, lambda i, *_: (0, 0), pipeline_mode=pl.Buffered(1))
    narrow = pl.BlockSpec((ROWS, features), lambda i, *_: (i, 0))
    broad = pl.BlockSpec((ROWS, wide), lambda i, *_: (i, 0))
    turned = pl.BlockSpec((features, ROWS), lambda i, *_: (0, i))
    shape = jax.ShapeDtypeStruct
    return pl.pallas_call(
        lambda *refs: ffn_kernel(*refs, seq_len=seq_len),
        grid_spec=pltpu.PrefetchScalarGridSpec(
            num_scalar_prefetch=2,
            grid=(total // ROWS,),
            in_specs=[turned, narrow, narrow, *weight_view(view, 3, features), whole(w_u), whole(w_d), whole(vec), whole(v_up)],
            out_specs=[
                narrow, narrow, broad, narrow, broad, narrow, narrow, turned,
                pl.BlockSpec((8, features), lambda i, *_: (0, 0)),
                pl.BlockSpec((1, wide), lambda i, *_: (0, 0)),
            ],
            scratch_shapes=[pltpu.VMEM((ROWS, wide), f32)],
        ),
        out_shape=[
            shape((total, features), bf), shape((total, features), bf), shape((total, wide), bf),
            shape((total, features), bf), shape((total, wide), bf), shape((total, features), f32),
            shape((total, features), bf), shape((features, total), bf),
            shape((8, features), f32), shape((1, wide), f32),
        ],
        compiler_params=pltpu.CompilerParams(vmem_limit_bytes=VMEM_LIMIT),
        cost_estimate=pl.CostEstimate(
            flops=2 * total * features * (4 * wide + 2 * features),
            bytes_accessed=2 * (2 * features * wide + 2 * total * wide + 8 * total * features),
            transcendentals=2 * total * wide),
    )(boundary, core, context_t, tokens, out_grad, *view[:2], w_u, w_d, vec, v_up)


def outer_kernel(active_ref, grad_ffn_ref, hidden_ref, grad_raised_ref, out_ref):
    parts, devices, cut, features = out_ref.shape
    step = pl.program_id(0)
    half = pl.num_programs(0) // 2

    @pl.when(step < half)
    def _():
        for f in range(devices):
            at = slice(f * parts * cut, (f + 1) * parts * cut)
            values = tn(active_ref[:, at], grad_ffn_ref[...]).astype(bf)
            for k in range(parts):
                out_ref[k, f] = values[k * cut : (k + 1) * cut, :]

    @pl.when(step >= half)
    def _():
        for k in range(parts):
            values = tn(hidden_ref[...], grad_raised_ref[:, k * features : (k + 1) * features]).astype(bf)
            for f in range(devices):
                out_ref[k, f] = values[f * cut : (f + 1) * cut, :]


def outer(active, grad_ffn, hidden, grad_raised, devices):
    total, features = hidden.shape
    wide = active.shape[1]
    parts, cut = wide // features, features // devices
    blocks = 2
    fixed = lambda a: pl.BlockSpec(a.shape, lambda i: (0, 0), pipeline_mode=pl.Buffered(1))
    return pl.pallas_call(
        outer_kernel,
        grid=(2 * blocks,),
        in_specs=[
            pl.BlockSpec((total, wide // blocks), lambda i: (0, jnp.minimum(i, blocks - 1))), fixed(grad_ffn),
            pl.BlockSpec((total, features // blocks), lambda i: (0, jnp.maximum(i - blocks, 0))), fixed(grad_raised)],
        out_specs=pl.BlockSpec((parts, devices // blocks, cut, features), lambda i: (i // blocks, i % blocks, 0, 0)),
        out_shape=jax.ShapeDtypeStruct((2 * parts, devices, cut, features), bf),
        compiler_params=pltpu.CompilerParams(vmem_limit_bytes=VMEM_LIMIT),
        cost_estimate=pl.CostEstimate(
            flops=4 * total * features * wide, bytes_accessed=4 * wide * (features + total), transcendentals=0),
    )(active, grad_ffn, hidden, grad_raised)


TILE = 16
WAIT_FOR = 2


def swap_core(a):
    n = lax.axis_size("fsdp")
    return lax.ppermute(a, "fsdp", [(i, i ^ 1) for i in range(n)])


def swap_line(a):
    n = lax.axis_size("fsdp")
    groups = [list(range(c, n, 2)) for c in range(2)]
    return lax.all_to_all(a, "fsdp", 0, 0, tiled=True, axis_index_groups=groups)


def along_line(a, step):
    n = lax.axis_size("fsdp")
    return lax.ppermute(a, "fsdp", [(i, i + 2 * step) for i in range(n) if 0 <= i + 2 * step < n])


def swap_rep(a):
    return lax.all_to_all(a, "rep", 0, 0, tiled=True)


def flip_rep(a, bit):
    return lax.ppermute(a, "rep", [(i, i ^ bit) for i in range(lax.axis_size("rep"))])


def after(a, *others):
    return lax.optimization_barrier((a,) + others)[0]


def spread(a, copies):
    return jnp.broadcast_to(a[None], (copies,) + a.shape)


def gather_rep(a):
    reps = lax.axis_size("rep")
    bits = [1 << k for k in range(reps.bit_length() - 1)]
    width = a.shape[-1] // len(bits)
    me = lax.axis_index("rep")
    shares = []
    for k in range(len(bits)):
        share = a[None, ..., k * width : (k + 1) * width]
        order = bits[k:] + bits[:k]
        for bit in order:
            other = flip_rep(share, bit)
            high = (me // bit) % 2 == 1
            share = jnp.concatenate([jnp.where(high, other, share), jnp.where(high, share, other)])
        at = np.zeros(reps, np.int32)
        for place in range(reps):
            rep = sum(bit for i, bit in enumerate(order) if (place >> i) & 1)
            at[rep] = place
        shares.append(jnp.stack([share[int(p)] for p in at]))
    return jnp.concatenate(shares, axis=-1)


def gather_parts(mine, shard, *others):
    places = lax.axis_size("fsdp") // 2
    place = lax.axis_index("fsdp") // 2
    steps = [k for d in range(1, places) for k in (d, -d)]
    seen = {-k: along_line(mine, k) for k in steps}
    near = min(WAIT_FOR, places - 1)
    seen[near], seen[-near], *others = lax.optimization_barrier((seen[near], seen[-near], *others))
    line = jnp.stack([seen[k] for k in range(1 - places, places) if k])
    line = lax.dynamic_slice_in_dim(line, places - 1 - place, places - 1, 0)
    every = gather_rep(line)
    at = jnp.arange(places)[:, None, None, None]
    every = every.swapaxes(0, 1)
    before = jnp.pad(every, ((0, 1), (0, 0), (0, 0), (0, 0)))
    behind = jnp.pad(every, ((1, 0), (0, 0), (0, 0), (0, 0)))
    every = jnp.where(at == place, shard[None], jnp.where(at < place, before, behind))
    other = swap_core(every)
    return every, other, others


def summed_over(a):
    return jnp.sum(a.astype(f32), 0).astype(bf)


def pad_tail(a, rows, columns):
    return jnp.pad(a, [(0, 0)] * (a.ndim - 2) + [(0, rows - a.shape[-2]), (0, columns - a.shape[-1])])


def per_device(
    tokens, lengths, boundary,
    w_query, b_query, w_key, b_key, w_value, b_value, w_out, b_out,
    first_gain, first_shift, w_up, b_up, w_down, b_down,
    second_gain, second_shift, rel_table, type_table, out_grad,
):
    micros, seqs, seq_len, features = tokens.shape
    rows = micros * seqs * seq_len
    heads = features // HEAD_DIM
    fs, reps = lax.axis_size("fsdp"), lax.axis_size("rep")
    places = fs // 2
    cut = w_query.shape[0]
    unit = 4 * cut // reps
    table_cut = rel_table.shape[0] // reps
    up_parts = w_up.shape[1] // features
    vectors = jnp.stack([b_query, b_key, b_value, b_out, first_gain, first_shift, b_down, second_gain,
                         second_shift, type_table[0], type_table[1]] + [b_up[k * cut : (k + 1) * cut] for k in range(up_parts)])
    vector_count = vectors.shape[0]
    vector_rows = -(-vector_count // TILE) * TILE
    vectors = pad_tail(vectors, vector_rows, features)
    shard = jnp.concatenate([
        jnp.stack([w_query, w_key, w_value, w_out]).reshape(reps, unit, features),
        rel_table.reshape(reps, table_cut, features),
        spread(vectors, reps)], axis=1)
    mine = lax.dynamic_index_in_dim(shard, lax.axis_index("rep"), 0, keepdims=False)
    own, other, (w_up, w_down) = gather_parts(mine, shard, w_up, w_down)
    w_u = lax.all_gather(w_up, "fsdp", axis=0, tiled=True)
    w_d = lax.all_gather(w_down, "fsdp", axis=0, tiled=True)
    direct = unit if unit == cut and cut % TILE == 0 and table_cut % TILE == 0 else 0
    part = unit + table_cut + vector_rows
    core = lax.axis_index("fsdp") % 2
    first = jnp.stack([jnp.where(core == 0, own, other), jnp.where(core == 0, other, own)], axis=1)
    if direct:
        view = (own, other, cut, own, other, (places, reps, table_cut, features), (0, 0, unit // table_cut, 0))
    else:
        four = first[:, :, :, :unit].reshape(fs, 4, reps // 4, unit, features).transpose(1, 0, 2, 3, 4)
        four = four.reshape(1, 4, features, features)
        rel = first[:, :, :, unit : unit + table_cut].reshape(1, 1, -1, features)
        view = (four, four, features, rel, rel, rel.shape, (0,) * 4)
    vector_at = slice(unit + table_cut, unit + table_cut + vector_count)
    wide = [a[:, 0, vector_at, :cut] for a in (own, other)]
    wide = jnp.stack([jnp.where(core == 0, *wide), jnp.where(core == 0, *wide[::-1])], axis=1)
    wide = wide.reshape(fs, vector_count, cut)
    core = core.reshape(1)
    wide = wide.transpose(1, 0, 2).astype(f32)
    v_up = wide[vector_count - up_parts :].transpose(1, 0, 2).reshape(1, -1)
    wide = wide.reshape(vector_count, features)

    offsets = np.clip(np.arange(2 * seq_len) - (seq_len - 1), 1 - seq_len, seq_len - 1)
    pick = pick_rows(offsets)
    pick_back = pick_rows(-offsets)
    flat_bound, flat_lengths = boundary.reshape(-1), lengths.reshape(-1)
    flat_tokens, flat_grad = tokens.reshape(rows, features), out_grad.reshape(rows, features)
    queries, keys, values, key_rows, query_rows, key_back_t, query_t, summed_low = project(
        flat_bound, core, flat_tokens, view, jnp.asarray(pick, bf), jnp.asarray(pick.T, bf), jnp.asarray(pick_back.T, bf),
        wide, wide[9:11], seq_len)
    context_t, probs, inverse_total = attn_fwd(
        queries, keys, values, key_back_t, query_t, flat_lengths, heads)
    (layer_out, hidden_low, active, grad_ffn, grad_raised, grad_first, grad_attended, grad_context_t,
     sums, sum_up) = ffn(flat_bound, core, context_t, flat_tokens, flat_grad, view, w_u, w_d, wide, v_up, seq_len)
    d_ffn = outer(active, grad_ffn, hidden_low, grad_raised, fs)
    early = lax.psum_scatter(d_ffn.reshape(-1, features, features), "fsdp", scatter_dimension=1, tiled=True)
    d_query, d_key, d_value, key_off, query_off = attn_bwd(
        queries, keys, values, grad_context_t, probs, inverse_total, key_rows, query_rows)
    made = unproject(
        flat_bound, core, summed_low, d_query, d_key, d_value, key_off, query_off, view,
        jnp.asarray(pick.T, bf), context_t, grad_attended, sums, sum_up, seq_len, direct,
        (reps, places, part, features))
    tokens_grad = token_grads(core, d_query, d_key, d_value, view, grad_first)
    if direct:
        keep, give = made
    else:
        four, d_rel, small = made
        four = four.reshape(4, places, 2, reps // 4, unit, features).transpose(0, 3, 1, 2, 4, 5)
        small = jnp.broadcast_to(small.astype(bf), (reps, places, 2) + small.shape)
        last = jnp.concatenate([
            four.reshape(reps, places, 2, unit, features),
            d_rel.reshape(places, 2, reps, table_cut, features).transpose(2, 0, 1, 3, 4), small], axis=3)
        keep = lax.dynamic_index_in_dim(last, core[0], 2, keepdims=False)
        give = lax.dynamic_index_in_dim(last, 1 - core[0], 2, keepdims=False)
    last = (keep.astype(f32) + swap_core(give).astype(f32)).astype(bf)
    early = lax.psum_scatter(early.reshape(-1, features), "rep", scatter_dimension=0, tiled=True)
    last = summed_over(swap_rep(last))
    early = after(early, last)
    early = lax.all_gather(early, "rep", axis=0, tiled=True)
    last = summed_over(swap_line(last))
    small = last[unit + table_cut : unit + table_cut + vector_count].astype(f32)
    small = lax.dynamic_slice_in_dim(small[: vector_count - up_parts], lax.axis_index("fsdp") * cut, cut, 1)
    d_b_up = last[unit + table_cut + vector_count - up_parts : unit + table_cut + vector_count].astype(f32)
    d_b_up = lax.dynamic_slice_in_dim(d_b_up.reshape(-1), lax.axis_index("fsdp") * up_parts * cut, up_parts * cut, 0)
    both = swap_rep(spread(last[: unit + table_cut], reps)).astype(f32)
    four = both[:, :unit].reshape(4, cut, features)
    s_q, s_k, s_v, s_o = four[0], four[1], four[2], four[3]
    s_rel = both[:, unit:].reshape(-1, features)
    (d_b_query, d_b_key, d_b_value, d_b_out, d_first_gain, d_first_shift, d_b_down,
     d_second_gain, d_second_shift, d_type_zero, d_type_one) = [
        small[k] for k in range(vector_count - up_parts)]
    s_down = early[: w_down.shape[0]].astype(f32)
    s_up = early[w_down.shape[0] :].reshape(up_parts, cut, features).transpose(1, 0, 2)
    s_up = s_up.reshape(cut, -1).astype(f32)
    return (
        layer_out.reshape(tokens.shape), tokens_grad.reshape(tokens.shape),
        s_q, d_b_query, s_k, d_b_key, s_v, d_b_value, s_o, d_b_out,
        d_first_gain, d_first_shift, s_up, d_b_up, s_down, d_b_down,
        d_second_gain, d_second_shift, s_rel, jnp.stack([d_type_zero, d_type_one]),
    )


def solution(mesh):
    seq = P(None, ("rep", "fsdp"), None, None)
    flat = P(None, ("rep", "fsdp"))
    mat, vec = P("fsdp", None), P("fsdp")
    weights = (mat, vec, mat, vec, mat, vec, mat, vec, vec, vec, mat, vec, mat, vec, vec, vec, mat,
               P(None, "fsdp"))
    return jax.shard_map(
        per_device,
        mesh=mesh,
        in_specs=(seq, flat, flat) + weights + (seq,),
        out_specs=(seq, seq) + weights,
        check_vma=False,
    )
```
